512 devices in a mesh: node: 64 (over z, x, core), tensor: 8 (over y).
Axes of the slice: x: 4, y: 8, z: 8, core: 2. Of those that a mesh axis runs over, the one named last changes fastest.
Arguments:
- inputs: bfloat16 [8192, 16384], P('node', 'tensor'), may hold values from -6 to 6
- upstream: bfloat16 [8192, 16384], P('node', 'tensor'), may hold values from -6 to 6
- token_adapter_index: int32 [8192], P('node'), may hold values from 0 to 1, as said below
- down_matrices: float32 [2, 16384, 32], P(None, ('tensor', 'node')), may hold values from -6 to 6
- up_matrices: float32 [2, 32, 16384], P(None, None, ('tensor', 'node')), may hold values from -6 to 6
- down_first_moment: float32 [2, 16384, 32], P(None, ('tensor', 'node')), may hold values from -6 to 6
- down_second_moment: float32 [2, 16384, 32], P(None, ('tensor', 'node')), may hold values from 0.5 to 8
- up_first_moment: float32 [2, 32, 16384], P(None, None, ('tensor', 'node')), may hold values from -6 to 6
- up_second_moment: float32 [2, 32, 16384], P(None, None, ('tensor', 'node')), may hold values from 0.5 to 8
Outputs:
- grad_inputs: bfloat16 [8192, 16384], P('node', 'tensor')
- updated_down_matrices: float32 [2, 16384, 32], P(None, ('tensor', 'node'))
- updated_up_matrices: float32 [2, 32, 16384], P(None, None, ('tensor', 'node'))
The draws below stay inside these ranges and needn't reach their ends.
Inputs may be any that keep to these rules, and one draw needn't show every extreme that they name: `token_adapter_index`: constant over each aligned block of 128 rows, nondecreasing over the rows of one index of node, skewed towards a few adapters drawn from the seed; every adapter has at least one block.
All inputs are finite; a program needn't handle non-finite values.
Results may differ from the reference program's by a relative error of at most 0.0045.
The reference program's roundings to bfloat16 on the way (of `low` and `back`) count: a program that leaves them out, or rounds other values in their place, can miss the bound.
Values may be sent and summed in bfloat16 or wider, within the bound.
No kernel may reach another device: no remote copies, remote signals or barrier semaphores. Data moves between devices by JAX's collectives and lax.ppermute only.
A program may use at most 192 MiB of HBM per device.

```python
import math
import jax
import jax.numpy as jnp
from jax import lax

INPUT_WIDTH = 16384
OUTPUT_WIDTH = 16384
ADAPTER_RANK = 32
TILE = 128
ADAPTER_COUNT = 2
TOK_DEV = 128
TOKENS = 8192


def draw_token_adapter_index(key, part):
    key = jax.random.fold_in(key, 11)
    first_key, second_key, order_key, place_key = jax.random.split(key, 4)
    block_count = TOKENS // TILE
    first = jax.random.randint(first_key, (block_count,), 0, ADAPTER_COUNT)
    second = jax.random.randint(second_key, (block_count,), 0, ADAPTER_COUNT)
    skewed = jnp.minimum(first, second)
    order = jax.random.permutation(order_key, ADAPTER_COUNT)
    labels = order[skewed]
    spots = jnp.arange(block_count)
    labels = jnp.where(spots < ADAPTER_COUNT, spots % ADAPTER_COUNT, labels)
    labels = labels[jax.random.permutation(place_key, block_count)]
    labels = jnp.sort(labels.reshape(TOKENS // TOK_DEV, TOK_DEV // TILE), axis=1)
    return jnp.repeat(labels.reshape(-1), TILE).astype(jnp.int32)


def block_scale(rng, extent, shards, low, largest):
    def one(dim, parts):
        steps = jax.random.uniform(jax.random.fold_in(jax.random.fold_in(rng, 6), dim), (parts,), jnp.float32, low / len(shards), largest / len(shards))
        return jnp.repeat(jnp.exp(steps), extent[dim] // parts).reshape((-1,) + (1,) * (len(extent) - dim - 1))

    loudness = one(*shards[0])
    for cut in shards[1:]:
        loudness = loudness * one(*cut)
    return loudness


def normal_values(stream_key, dims, width, most, cuts=(), dtype=jnp.bfloat16):
    factor_of = block_scale(stream_key, dims, cuts, -0.22, 0.18) if cuts else 1.0
    result = jax.random.normal(stream_key, dims, jnp.float32) * width * factor_of
    return jnp.minimum(jnp.maximum(result, -most), most).astype(dtype)


def setup_inputs(seed: int = 0) -> dict:
    key_of = jax.random.split(jax.random.key(seed), 10)
    inputs = normal_values(key_of[0], (TOKENS, INPUT_WIDTH), 1.0, 6.0, ((0, 64), (1, 8)))
    upstream = normal_values(key_of[1], (TOKENS, OUTPUT_WIDTH), 1.0, 6.0, ((0, 64), (1, 8)))
    token_adapter_index = draw_token_adapter_index(jax.random.fold_in(key_of[9], 71), 0)
    down_matrices = normal_values(key_of[3], (ADAPTER_COUNT, INPUT_WIDTH, ADAPTER_RANK), 1.0, 6.0, ((1, 512),), jnp.float32)
    up_matrices = normal_values(key_of[4], (ADAPTER_COUNT, ADAPTER_RANK, OUTPUT_WIDTH), 1.0, 6.0, ((2, 512),), jnp.float32)
    down_first_moment = normal_values(key_of[5], (ADAPTER_COUNT, INPUT_WIDTH, ADAPTER_RANK), 1.0, 6.0, ((1, 512),), jnp.float32)
    down_second_moment = jnp.clip(jnp.exp(math.log(8.0) - 2.7725887 * jax.random.uniform(key_of[6], (ADAPTER_COUNT, INPUT_WIDTH, ADAPTER_RANK), jnp.float32) ** block_scale(key_of[6], (ADAPTER_COUNT, INPUT_WIDTH, ADAPTER_RANK), ((1, 512),), -0.2, 0.2)), 0.5, 8.0)
    up_first_moment = normal_values(key_of[7], (ADAPTER_COUNT, ADAPTER_RANK, OUTPUT_WIDTH), 1.0, 6.0, ((2, 512),), jnp.float32)
    up_second_moment = jnp.clip(jnp.exp(math.log(8.0) - 2.7725887 * jax.random.uniform(key_of[8], (ADAPTER_COUNT, ADAPTER_RANK, OUTPUT_WIDTH), jnp.float32) ** block_scale(key_of[8], (ADAPTER_COUNT, ADAPTER_RANK, OUTPUT_WIDTH), ((2, 512),), -0.2, 0.2)), 0.5, 8.0)
    return {"inputs": inputs, "upstream": upstream, "token_adapter_index": token_adapter_index, "down_matrices": down_matrices, "up_matrices": up_matrices, "down_first_moment": down_first_moment, "down_second_moment": down_second_moment, "up_first_moment": up_first_moment, "up_second_moment": up_second_moment}


beta_one = 0.9
beta_two = 0.95
learn_rate = 0.3
adam_eps = 1e-08
step_number = 10

def moment_optimizer_step(weights, grads, moment, second):
    fresh_moment = beta_one * moment + (1.0 - beta_one) * grads
    fresh_second = beta_two * second + (1.0 - beta_two) * grads * grads
    first_fix = 1.0 - beta_one ** step_number
    second_fix = 1.0 - beta_two ** step_number
    return weights - learn_rate * (fresh_moment / first_fix) / (jnp.sqrt(fresh_second / second_fix) + adam_eps)

def reference(inputs, upstream, token_adapter_index, down_matrices, up_matrices, down_first_moment, down_second_moment, up_first_moment, up_second_moment):
    scale_in = INPUT_WIDTH ** (-0.5)
    scale_rank = ADAPTER_RANK ** (-0.5)
    down_half_block = down_matrices.astype(jnp.bfloat16)
    up_half_block = up_matrices.astype(jnp.bfloat16)
    tile_count = TOKENS // TILE
    x_tiles = inputs.reshape(tile_count, TILE, INPUT_WIDTH)
    d_tiles = upstream.reshape(tile_count, TILE, OUTPUT_WIDTH)
    tile_ids = token_adapter_index.reshape(tile_count, TILE)[:, 0].astype(jnp.int32)

    def one_tile(totals, pieces):
        down_gradient, up_gradient = totals
        x_rows, d_rows, adapter_now = pieces
        a_tile = down_half_block[adapter_now]
        b_tile = up_half_block[adapter_now]
        low = (jnp.dot(x_rows, a_tile, preferred_element_type=jnp.float32) * scale_in).astype(jnp.bfloat16)
        back = (jnp.dot(d_rows, b_tile.T, preferred_element_type=jnp.float32) * scale_rank).astype(jnp.bfloat16)
        grad_in = (jnp.dot(back, a_tile.T, preferred_element_type=jnp.float32) * scale_in).astype(jnp.bfloat16)
        term_a = jnp.dot(x_rows.T, back, preferred_element_type=jnp.float32) * scale_in
        term_b = jnp.dot(low.T, d_rows, preferred_element_type=jnp.float32) * scale_rank
        down_gradient = down_gradient.at[adapter_now].add(term_a)
        up_gradient = up_gradient.at[adapter_now].add(term_b)
        return ((down_gradient, up_gradient), grad_in)
    slice_offset = (jnp.zeros(down_matrices.shape, jnp.float32), jnp.zeros(up_matrices.shape, jnp.float32))
    (down_gradient, up_gradient), grad_in = lax.scan(one_tile, slice_offset, (x_tiles, d_tiles, tile_ids))
    updated_down_matrices = moment_optimizer_step(down_matrices, down_gradient, down_first_moment, down_second_moment)
    updated_up_matrices = moment_optimizer_step(up_matrices, up_gradient, up_first_moment, up_second_moment)
    return (grad_in.reshape(TOKENS, INPUT_WIDTH), updated_down_matrices, updated_up_matrices)
```

```python
import jax
import jax.numpy as jnp
from jax import lax
from jax.experimental import pallas as pl
from jax.experimental.pallas import tpu as pltpu
from jax.sharding import PartitionSpec as P

INPUT_WIDTH = 16384
ADAPTER_RANK = 32

beta_one = 0.9
beta_two = 0.95
learn_rate = 0.3
adam_eps = 1e-08
step_number = 10

F32 = jnp.float32
BF16 = jnp.bfloat16
VMEM = pl.BlockSpec(memory_space=pltpu.VMEM)
SCALE_IN = INPUT_WIDTH ** (-0.5)
SCALE_RANK = ADAPTER_RANK ** (-0.5)


def moment_optimizer_step(weights, grads, moment, second):
    fresh_moment = beta_one * moment + (1.0 - beta_one) * grads
    fresh_second = beta_two * second + (1.0 - beta_two) * grads * grads
    first_fix = 1.0 - beta_one**step_number
    second_fix = 1.0 - beta_two**step_number
    return weights - learn_rate * (fresh_moment / first_fix) / (
        jnp.sqrt(fresh_second / second_fix) + adam_eps
    )


def pack_kernel(ids_ref, down_ref, up_ref, out_ref):
    down = down_ref[...].astype(BF16)
    up = up_ref[...]
    rows = jnp.concatenate(
        [down[0], down[1], up[0].T.astype(BF16), up[1].T.astype(BF16)], axis=1
    )
    depth = rows.shape[0]
    peers = out_ref.shape[0]
    out_ref[:, :depth, :] = jnp.broadcast_to(rows[None], (peers,) + rows.shape)
    spare = out_ref.shape[1] - depth
    mark = jnp.broadcast_to(ids_ref[...].astype(F32), (spare, 128)).astype(BF16)
    out_ref[:, depth:, :] = jnp.broadcast_to(mark[None], (peers, spare, 128))


def partial_kernel(ids_ref, table_ref, x_ref, d_ref, out_ref, owner_ref):
    peers, rows, _ = table_ref.shape
    depth = x_ref.shape[1] // peers
    table = table_ref[:, :depth, :].reshape(peers * depth, 128)
    owner_ref[...] = table_ref[:, depth : depth + 1, :].astype(F32)
    low = jnp.dot(x_ref[...], table, preferred_element_type=F32)
    back = jnp.dot(d_ref[...], table, preferred_element_type=F32)
    lane = lax.broadcasted_iota(jnp.int32, low.shape, 1)
    both = jnp.where(lane < 64, low, back).T
    first = ids_ref[...] == 0
    low = jnp.where(first, both[0:32], both[32:64])
    back = jnp.where(first, both[64:96], both[96:128])
    sums = jnp.concatenate([low, back], axis=0).astype(BF16)
    out_ref[...] = jnp.broadcast_to(sums[None], out_ref.shape)


def full_sums(sums_ref):
    total = jnp.sum(sums_ref[...].astype(F32), axis=0)
    low = (total[0:32] * SCALE_IN).astype(BF16).astype(F32)
    back = (total[32:64] * SCALE_RANK).astype(BF16).astype(F32)
    return low, back


def gradient_kernel(sums_ref, x_ref, d_ref, out_ref):
    low, back = full_sums(sums_ref)
    none = jnp.zeros_like(low)
    from_x = jnp.concatenate([back, none, back, none], axis=0).astype(BF16)
    from_d = jnp.concatenate([none, low, none, low], axis=0).astype(BF16)
    wide = jnp.dot(from_x, x_ref[...], preferred_element_type=F32)
    wide = wide + jnp.dot(from_d, d_ref[...], preferred_element_type=F32)
    row = lax.broadcasted_iota(jnp.int32, (128, 1), 0)
    wide = wide * jnp.where((row // 32) % 2 == 0, SCALE_IN, SCALE_RANK)
    peers, half, _ = out_ref.shape
    tall = wide.T.reshape(peers, 2, half, 128)
    lane = lax.broadcasted_iota(jnp.int32, (1, 1, 128), 2)
    out_ref[...] = jnp.where(lane < 64, tall[:, 0], tall[:, 1]).astype(BF16)


def grad_input_kernel(ids_ref, sums_ref, table_ref, out_ref):
    _, back = full_sums(sums_ref)
    first = ids_ref[...] == 0
    none = jnp.zeros_like(back)
    placed = jnp.concatenate(
        [jnp.where(first, back, none), jnp.where(first, none, back), none, none], axis=0
    )
    peers = table_ref.shape[0]
    depth = out_ref.shape[1] // peers
    table = table_ref[:, :depth, :].reshape(peers * depth, 128)
    grad = lax.dot_general(
        placed.T.astype(BF16), table, (((1,), (1,)), ((), ())), preferred_element_type=F32
    )
    out_ref[...] = (grad * SCALE_IN).astype(BF16)


def update_kernel(
    owner_ref, terms_ref, wd_ref, wu_ref, md_ref, vd_ref, mu_ref, vu_ref, down_ref, up_ref
):
    terms = terms_ref[...].astype(F32)
    owner = owner_ref[...]
    for adapter in range(wd_ref.shape[0]):
        total = jnp.sum(jnp.where(owner == adapter, terms, 0.0), axis=0)
        grad_a = jnp.concatenate([total[:, 0:32], total[:, 64:96]], axis=0)
        grad_b = jnp.concatenate([total[:, 32:64], total[:, 96:128]], axis=0).T
        down_ref[adapter] = moment_optimizer_step(
            wd_ref[adapter], grad_a, md_ref[adapter], vd_ref[adapter]
        )
        up_ref[adapter] = moment_optimizer_step(
            wu_ref[adapter], grad_b, mu_ref[adapter], vu_ref[adapter]
        )


def call(kernel, out_shape, *args):
    many = isinstance(out_shape, tuple)
    return pl.pallas_call(
        kernel,
        out_shape=out_shape,
        in_specs=[VMEM] * len(args),
        out_specs=(VMEM,) * len(out_shape) if many else VMEM,
        compiler_params=pltpu.CompilerParams(vmem_limit_bytes=32 * 2**20),
    )(*args)


def shape(dims, dtype):
    return jax.ShapeDtypeStruct(dims, dtype)


def exchange(blocks, axis):
    return lax.all_to_all(blocks, axis, split_axis=0, concat_axis=0, tiled=True)


def local(
    inputs,
    upstream,
    token_adapter_index,
    down_matrices,
    up_matrices,
    down_first_moment,
    down_second_moment,
    up_first_moment,
    up_second_moment,
):
    nodes = lax.axis_size("node")
    shards = lax.axis_size("tensor")
    depth = down_matrices.shape[1]
    ids = token_adapter_index.reshape(1, 128)
    packed = call(
        pack_kernel, shape((nodes, depth + 8, 128), BF16), ids, down_matrices, up_matrices
    )
    table = exchange(packed, "node")
    parts, owner = call(
        partial_kernel,
        (shape((shards, 64, 128), BF16), shape((nodes, 1, 128), F32)),
        ids,
        table,
        inputs,
        upstream,
    )
    sums = exchange(parts, "tensor")
    terms = call(
        gradient_kernel, shape((nodes, depth // 2, 128), BF16), sums, inputs, upstream
    )
    terms = exchange(terms, "node")
    grad_in = call(grad_input_kernel, shape(inputs.shape, BF16), ids, sums, table)
    down, up = call(
        update_kernel,
        (shape(down_matrices.shape, F32), shape(up_matrices.shape, F32)),
        owner,
        terms,
        down_matrices,
        up_matrices,
        down_first_moment,
        down_second_moment,
        up_first_moment,
        up_second_moment,
    )
    return (grad_in, down, up)


def solution(mesh):
    return jax.shard_map(
        local,
        mesh=mesh,
        in_specs=(
            P("node", "tensor"),
            P("node", "tensor"),
            P("node"),
            P(None, ("tensor", "node"), None),
            P(None, None, ("tensor", "node")),
            P(None, ("tensor", "node"), None),
            P(None, ("tensor", "node"), None),
            P(None, None, ("tensor", "node")),
            P(None, None, ("tensor", "node")),
        ),
        out_specs=(
            P("node", "tensor"),
            P(None, ("tensor", "node"), None),
            P(None, None, ("tensor", "node")),
        ),
        check_vma=False,
    )
```

```python
import jax
import jax.numpy as jnp
from jax import lax
from jax.experimental import pallas as pl
from jax.experimental.pallas import tpu as pltpu
from jax.sharding import PartitionSpec as P

INPUT_WIDTH = 16384
ADAPTER_RANK = 32

beta_one = 0.9
beta_two = 0.95
learn_rate = 0.3
adam_eps = 1e-08
step_number = 10

F32 = jnp.float32
BF16 = jnp.bfloat16
VMEM = pl.BlockSpec(memory_space=pltpu.VMEM)
SCALE_IN = INPUT_WIDTH ** (-0.5)
SCALE_RANK = ADAPTER_RANK ** (-0.5)


def moment_optimizer_step(weights, grads, moment, second):
    fresh_moment = beta_one * moment + (1.0 - beta_one) * grads
    fresh_second = beta_two * second + (1.0 - beta_two) * grads * grads
    first_fix = 1.0 - beta_one**step_number
    second_fix = 1.0 - beta_two**step_number
    return weights - learn_rate * (fresh_moment / first_fix) / (
        jnp.sqrt(fresh_second / second_fix) + adam_eps
    )


def pack_kernel(ids_hbm, down_hbm, up_hbm, out_ref, ids_ref, down_ref, up_ref, sems):
    loads = [
        pltpu.make_async_copy(ids_hbm, ids_ref, sems.at[0]),
        pltpu.make_async_copy(down_hbm, down_ref, sems.at[1]),
        pltpu.make_async_copy(up_hbm, up_ref, sems.at[2]),
    ]
    for load in loads:
        load.start()
    for load in loads:
        load.wait()
    down = down_ref[...].astype(BF16)
    up = up_ref[...]
    rows = jnp.concatenate(
        [down[0], down[1], up[0].T.astype(BF16), up[1].T.astype(BF16)], axis=1
    )
    depth = rows.shape[0]
    peers = out_ref.shape[0]
    out_ref[:, :depth, :] = jnp.broadcast_to(rows[None], (peers,) + rows.shape)
    spare = out_ref.shape[1] - depth
    mark = jnp.broadcast_to(ids_ref[...].astype(F32), (spare, 128)).astype(BF16)
    out_ref[:, depth:, :] = jnp.broadcast_to(mark[None], (peers, spare, 128))


def partial_kernel(ids_ref, own_ref, other_ref, x_ref, d_ref, out_ref, owner_ref, table_ref):
    core = lax.axis_index("node") % 2
    pairs, _, depth, _ = table_ref.shape
    table_ref[:, core] = own_ref[:, :depth, :]
    table_ref[:, 1 - core] = other_ref[:, :depth, :]
    owner_ref[:, core] = own_ref[:, depth : depth + 1, :].astype(F32)
    owner_ref[:, 1 - core] = other_ref[:, depth : depth + 1, :].astype(F32)
    table = table_ref[...].reshape(pairs * 2 * depth, 128)
    low = jnp.dot(x_ref[...], table, preferred_element_type=F32)
    back = jnp.dot(d_ref[...], table, preferred_element_type=F32)
    lane = lax.broadcasted_iota(jnp.int32, low.shape, 1)
    both = jnp.where(lane < 64, low, back).T
    first = ids_ref[...] == 0
    low = jnp.where(first, both[0:32], both[32:64])
    back = jnp.where(first, both[64:96], both[96:128])
    sums = jnp.concatenate([low, back], axis=0).astype(BF16)
    out_ref[...] = jnp.broadcast_to(sums[None], out_ref.shape)


def full_sums(sums_ref):
    total = jnp.sum(sums_ref[...].astype(F32), axis=0)
    low = (total[0:32] * SCALE_IN).astype(BF16).astype(F32)
    back = (total[32:64] * SCALE_RANK).astype(BF16).astype(F32)
    return low, back


def gradient_kernel(sums_ref, x_ref, d_ref, out_ref):
    low, back = full_sums(sums_ref)
    none = jnp.zeros_like(low)
    from_x = jnp.concatenate([back, none, back, none], axis=0).astype(BF16)
    from_d = jnp.concatenate([none, low, none, low], axis=0).astype(BF16)
    wide = jnp.dot(from_x, x_ref[...], preferred_element_type=F32)
    wide = wide + jnp.dot(from_d, d_ref[...], preferred_element_type=F32)
    row = lax.broadcasted_iota(jnp.int32, (128, 1), 0)
    wide = wide * jnp.where((row // 32) % 2 == 0, SCALE_IN, SCALE_RANK)
    peers, half, _ = out_ref.shape
    tall = wide.T.reshape(peers, 2, half, 128)
    lane = lax.broadcasted_iota(jnp.int32, (1, 1, 128), 2)
    out_ref[...] = jnp.where(lane < 64, tall[:, 0], tall[:, 1]).astype(BF16)


def grad_input_kernel(ids_ref, sums_ref, table_ref, out_ref):
    _, back = full_sums(sums_ref)
    first = ids_ref[...] == 0
    none = jnp.zeros_like(back)
    placed = jnp.concatenate(
        [jnp.where(first, back, none), jnp.where(first, none, back), none, none], axis=0
    )
    table = table_ref[...].reshape(out_ref.shape[1], 128)
    grad = lax.dot_general(
        placed.T.astype(BF16), table, (((1,), (1,)), ((), ())), preferred_element_type=F32
    )
    out_ref[...] = (grad * SCALE_IN).astype(BF16)


def update_kernel(
    owner_ref, terms_ref, wd_ref, wu_ref, md_ref, vd_ref, mu_ref, vu_ref, down_ref, up_ref
):
    terms = terms_ref[...].astype(F32)
    owner = owner_ref[...].reshape(terms.shape[0], 1, 128)
    for adapter in range(wd_ref.shape[0]):
        total = jnp.sum(jnp.where(owner == adapter, terms, 0.0), axis=0)
        grad_a = jnp.concatenate([total[:, 0:32], total[:, 64:96]], axis=0)
        grad_b = jnp.concatenate([total[:, 32:64], total[:, 96:128]], axis=0).T
        down_ref[adapter] = moment_optimizer_step(
            wd_ref[adapter], grad_a, md_ref[adapter], vd_ref[adapter]
        )
        up_ref[adapter] = moment_optimizer_step(
            wu_ref[adapter], grad_b, mu_ref[adapter], vu_ref[adapter]
        )


def call(kernel, out_shape, *args):
    many = isinstance(out_shape, tuple)
    return pl.pallas_call(
        kernel,
        out_shape=out_shape,
        in_specs=[VMEM] * len(args),
        out_specs=(VMEM,) * len(out_shape) if many else VMEM,
        compiler_params=pltpu.CompilerParams(vmem_limit_bytes=32 * 2**20),
    )(*args)


def shape(dims, dtype):
    return jax.ShapeDtypeStruct(dims, dtype)


def exchange(blocks, axis, groups=None):
    return lax.all_to_all(
        blocks, axis, split_axis=0, concat_axis=0, axis_index_groups=groups, tiled=True
    )


def local(
    inputs,
    upstream,
    token_adapter_index,
    down_matrices,
    up_matrices,
    down_first_moment,
    down_second_moment,
    up_first_moment,
    up_second_moment,
):
    nodes = lax.axis_size("node")
    shards = lax.axis_size("tensor")
    depth = down_matrices.shape[1]
    ids = token_adapter_index.reshape(1, 128)
    pairs = nodes // 2
    packed = pl.pallas_call(
        pack_kernel,
        out_shape=shape((pairs, depth + 8, 128), BF16),
        in_specs=[pl.BlockSpec(memory_space=pl.ANY)] * 3,
        out_specs=VMEM,
        scratch_shapes=[
            pltpu.VMEM(ids.shape, jnp.int32),
            pltpu.VMEM(down_matrices.shape, F32),
            pltpu.VMEM(up_matrices.shape, F32),
            pltpu.SemaphoreType.DMA((3,)),
        ],
        compiler_params=pltpu.CompilerParams(vmem_limit_bytes=60 * 2**20),
    )(ids, down_matrices, up_matrices)
    cores = [[2 * pair + core for pair in range(pairs)] for core in range(2)]
    own = exchange(packed, "node", cores)
    other = lax.ppermute(own, "node", [(node, node ^ 1) for node in range(nodes)])
    parts, owner, table = call(
        partial_kernel,
        (
            shape((shards, 64, 128), BF16),
            shape((pairs, 2, 1, 128), F32),
            shape((pairs, 2, depth, 128), BF16),
        ),
        ids,
        own,
        other,
        inputs,
        upstream,
    )
    sums = exchange(parts, "tensor")
    terms = call(
        gradient_kernel, shape((nodes, depth // 2, 128), BF16), sums, inputs, upstream
    )
    terms = exchange(terms, "node")
    grad_in = call(grad_input_kernel, shape(inputs.shape, BF16), ids, sums, table)
    down, up = call(
        update_kernel,
        (shape(down_matrices.shape, F32), shape(up_matrices.shape, F32)),
        owner,
        terms,
        down_matrices,
        up_matrices,
        down_first_moment,
        down_second_moment,
        up_first_moment,
        up_second_moment,
    )
    return (grad_in, down, up)


def solution(mesh):
    return jax.shard_map(
        local,
        mesh=mesh,
        in_specs=(
            P("node", "tensor"),
            P("node", "tensor"),
            P("node"),
            P(None, ("tensor", "node"), None),
            P(None, None, ("tensor", "node")),
            P(None, ("tensor", "node"), None),
            P(None, ("tensor", "node"), None),
            P(None, None, ("tensor", "node")),
            P(None, None, ("tensor", "node")),
        ),
        out_specs=(
            P("node", "tensor"),
            P(None, ("tensor", "node"), None),
            P(None, None, ("tensor", "node")),
        ),
        check_vma=False,
    )
```

```python
import functools

import jax
import jax.numpy as jnp
from jax import lax
from jax.experimental import pallas as pl
from jax.experimental.pallas import tpu as pltpu
from jax.sharding import PartitionSpec as P

INPUT_WIDTH = 16384
ADAPTER_RANK = 32

beta_one = 0.9
beta_two = 0.95
learn_rate = 0.3
adam_eps = 1e-08
step_number = 10

F32 = jnp.float32
BF16 = jnp.bfloat16
VMEM = pl.BlockSpec(memory_space=pltpu.VMEM)
SCALE_IN = INPUT_WIDTH ** (-0.5)
SCALE_RANK = ADAPTER_RANK ** (-0.5)
NEAR_FLOPS = 1e10


def moment_optimizer_step(weights, grads, moment, second):
    fresh_moment = beta_one * moment + (1.0 - beta_one) * grads
    fresh_second = beta_two * second + (1.0 - beta_two) * grads * grads
    first_fix = 1.0 - beta_one**step_number
    second_fix = 1.0 - beta_two**step_number
    return weights - learn_rate * (fresh_moment / first_fix) / (
        jnp.sqrt(fresh_second / second_fix) + adam_eps
    )


def pack_kernel(down_hbm, up_hbm, out_ref, down_ref, up_ref, sems):
    loads = [
        pltpu.make_async_copy(down_hbm, down_ref, sems.at[0]),
        pltpu.make_async_copy(up_hbm, up_ref, sems.at[1]),
    ]
    for load in loads:
        load.start()
    for load in loads:
        load.wait()
    down = down_ref[...].astype(BF16)
    up = up_ref[...]
    rows = jnp.concatenate(
        [down[0], down[1], up[0].T.astype(BF16), up[1].T.astype(BF16)], axis=1
    )
    out_ref[...] = jnp.broadcast_to(rows[None], out_ref.shape)


def turn_kernel(away, x_ref, d_ref, out_ref):
    core = lax.axis_index("node") % 2
    pairs, depth, _ = out_ref.shape
    for spot, piece_ref in enumerate((x_ref, d_ref)):
        span = slice(128 * spot, 128 * spot + 128)
        tall = piece_ref[...].T.reshape(pairs, 2, depth, 128)
        out_ref[:, :, span] = jnp.where(core == away, tall[:, 0], tall[:, 1])


def products(table_ref, tile_ref):
    rows = tile_ref.shape[0] * tile_ref.shape[1]
    wide = lax.dot_general(
        table_ref[...].reshape(rows, 128),
        tile_ref[...].reshape(rows, 256),
        (((0,), (0,)), ((), ())),
        preferred_element_type=F32,
    )
    return jnp.concatenate([wide[0:64, 0:128], wide[64:128, 128:256]], axis=0)


def near_kernel(ids_ref, table_ref, own_ref, other_ref, out_ref):
    out_ref[0:128, 0:128] = products(table_ref, own_ref)
    out_ref[0:128, 128:256] = products(table_ref, other_ref)
    out_ref[128:136] = jnp.broadcast_to(ids_ref[:, 0:1].astype(F32), (8, 256))


def partial_kernel(own_ref, other_ref, out_ref):
    tiles = (
        (own_ref[128:129, 0:128], own_ref[0:128, 0:128] + other_ref[0:128, 128:256]),
        (other_ref[128:129, 0:128], own_ref[0:128, 128:256] + other_ref[0:128, 0:128]),
    )
    parts = []
    for ids, both in tiles:
        first = ids == 0
        parts.append(jnp.where(first, both[0:32], both[32:64]))
        parts.append(jnp.where(first, both[64:96], both[96:128]))
    sums = jnp.concatenate(parts, axis=0).astype(BF16)
    out_ref[...] = jnp.broadcast_to(sums[None], out_ref.shape)


def full_sums(total):
    low = (total[0:32] * SCALE_IN).astype(BF16).astype(F32)
    back = (total[32:64] * SCALE_RANK).astype(BF16).astype(F32)
    return low, back


def by_adapter(ids, values):
    none = jnp.zeros_like(values)
    first = ids == 0
    return [jnp.where(first, values, none), jnp.where(first, none, values)]


def gradient_kernel(own_ids_ref, other_ids_ref, sums_ref, own_ref, other_ref, out_ref):
    total = jnp.sum(sums_ref[...].astype(F32), axis=0)
    pairs, depth, width = own_ref.shape
    grads = jnp.zeros((pairs * depth, 128), F32)
    tiles = ((own_ids_ref, own_ref), (other_ids_ref, other_ref))
    for spot, (ids_ref, tile_ref) in enumerate(tiles):
        ids = ids_ref[128:129, 0:128]
        low, back = full_sums(total[64 * spot : 64 * spot + 64])
        none = [jnp.zeros_like(low)] * 2
        from_x = jnp.concatenate(by_adapter(ids, back) + none, axis=0)
        from_d = jnp.concatenate(none + by_adapter(ids, low), axis=0)
        grads = grads + lax.dot_general(
            tile_ref[...].reshape(pairs * depth, width),
            jnp.concatenate([from_x, from_d], axis=1).astype(BF16),
            (((1,), (1,)), ((), ())),
            preferred_element_type=F32,
        )
    lane = lax.broadcasted_iota(jnp.int32, (1, 128), 1)
    grads = grads * jnp.where(lane < 64, SCALE_IN, SCALE_RANK)
    out_ref[...] = grads.astype(BF16).reshape(out_ref.shape)


def grad_input_kernel(ids_ref, sums_ref, own_ref, other_ref, out_ref, table_ref):
    core = lax.axis_index("node") % 2
    table_ref[:, core] = own_ref[...]
    table_ref[:, 1 - core] = other_ref[...]
    total = jnp.sum(sums_ref[:, 0:64, :].astype(F32), axis=0)
    _, back = full_sums(total)
    none = [jnp.zeros_like(back)] * 2
    placed = jnp.concatenate(by_adapter(ids_ref[...], back) + none, axis=0)
    table = table_ref[...].reshape(out_ref.shape[1], 128)
    grad = lax.dot_general(
        placed.T.astype(BF16), table, (((1,), (1,)), ((), ())), preferred_element_type=F32
    )
    out_ref[...] = (grad * SCALE_IN).astype(BF16)


def update_kernel(
    terms_ref, wd_ref, wu_ref, md_ref, vd_ref, mu_ref, vu_ref, down_ref, up_ref
):
    total = jnp.sum(terms_ref[...].astype(F32), axis=0)
    for adapter in range(wd_ref.shape[0]):
        grad_a = total[:, 32 * adapter : 32 * adapter + 32]
        grad_b = total[:, 64 + 32 * adapter : 96 + 32 * adapter].T
        down_ref[adapter] = moment_optimizer_step(
            wd_ref[adapter], grad_a, md_ref[adapter], vd_ref[adapter]
        )
        up_ref[adapter] = moment_optimizer_step(
            wu_ref[adapter], grad_b, mu_ref[adapter], vu_ref[adapter]
        )


def call(kernel, out_shape, *args, scratch=(), flops=0):
    many = isinstance(out_shape, tuple)
    return pl.pallas_call(
        kernel,
        out_shape=out_shape,
        in_specs=[VMEM] * len(args),
        out_specs=(VMEM,) * len(out_shape) if many else VMEM,
        scratch_shapes=scratch,
        compiler_params=pltpu.CompilerParams(vmem_limit_bytes=16 * 2**20),
        cost_estimate=pl.CostEstimate(flops=int(flops), bytes_accessed=2**20, transcendentals=0),
    )(*args)


def shape(dims, dtype):
    return jax.ShapeDtypeStruct(dims, dtype)


def exchange(blocks, axis, groups=None):
    return lax.all_to_all(
        blocks, axis, split_axis=0, concat_axis=0, axis_index_groups=groups, tiled=True
    )


def local(
    inputs,
    upstream,
    token_adapter_index,
    down_matrices,
    up_matrices,
    down_first_moment,
    down_second_moment,
    up_first_moment,
    up_second_moment,
):
    nodes = lax.axis_size("node")
    shards = lax.axis_size("tensor")
    depth = down_matrices.shape[1]
    pairs = nodes // 2
    cores = [[2 * pair + core for pair in range(pairs)] for core in range(2)]

    def swap(block):
        return lax.ppermute(block, "node", [(node, node ^ 1) for node in range(nodes)])

    ids = token_adapter_index.reshape(1, 128)
    packed = pl.pallas_call(
        pack_kernel,
        out_shape=pltpu.VMEM((pairs, depth, 128), BF16),
        in_specs=[pl.BlockSpec(memory_space=pl.ANY)] * 2,
        out_specs=VMEM,
        scratch_shapes=[
            pltpu.VMEM(down_matrices.shape, F32),
            pltpu.VMEM(up_matrices.shape, F32),
            pltpu.SemaphoreType.DMA((2,)),
        ],
        compiler_params=pltpu.CompilerParams(vmem_limit_bytes=16 * 2**20),
    )(
        pltpu.with_memory_space_constraint(down_matrices, pltpu.HBM),
        pltpu.with_memory_space_constraint(up_matrices, pltpu.HBM),
    )
    own = exchange(packed, "node", cores)
    rows, width = inputs.shape
    half = shape((pairs, depth, 2 * rows), BF16)
    near = call(functools.partial(turn_kernel, 0), half, inputs, upstream, flops=NEAR_FLOPS)
    far = call(functools.partial(turn_kernel, 1), half, inputs, upstream)
    beside = swap(far)
    halves = call(near_kernel, shape((136, 2 * rows), F32), ids, own, near, beside)
    others = swap(halves)
    parts = call(partial_kernel, shape((shards, 128, 128), BF16), halves, others)
    sums = exchange(parts, "tensor")
    other = swap(own)
    terms = call(
        gradient_kernel,
        shape((pairs, depth, 128), BF16),
        halves,
        others,
        sums,
        near,
        beside,
    )
    terms = exchange(terms, "node", cores)
    grad_in = call(
        grad_input_kernel,
        shape(inputs.shape, BF16),
        ids,
        sums,
        own,
        other,
        scratch=[pltpu.VMEM((pairs, 2, depth, 128), BF16)],
    )
    down, up = call(
        update_kernel,
        (shape(down_matrices.shape, F32), shape(up_matrices.shape, F32)),
        terms,
        down_matrices,
        up_matrices,
        down_first_moment,
        down_second_moment,
        up_first_moment,
        up_second_moment,
    )
    return (grad_in, down, up)


def solution(mesh):
    return jax.shard_map(
        local,
        mesh=mesh,
        in_specs=(
            P("node", "tensor"),
            P("node", "tensor"),
            P("node"),
            P(None, ("tensor", "node"), None),
            P(None, None, ("tensor", "node")),
            P(None, ("tensor", "node"), None),
            P(None, ("tensor", "node"), None),
            P(None, None, ("tensor", "node")),
            P(None, None, ("tensor", "node")),
        ),
        out_specs=(
            P("node", "tensor"),
            P(None, ("tensor", "node"), None),
            P(None, None, ("tensor", "node")),
        ),
        check_vma=False,
    )
```

```python
import functools

import jax
import jax.numpy as jnp
from jax import lax
from jax.experimental import pallas as pl
from jax.experimental.pallas import tpu as pltpu
from jax.sharding import PartitionSpec as P

INPUT_WIDTH = 16384
ADAPTER_RANK = 32

beta_one = 0.9
beta_two = 0.95
learn_rate = 0.3
adam_eps = 1e-08
step_number = 10

F32 = jnp.float32
BF16 = jnp.bfloat16
VMEM = pl.BlockSpec(memory_space=pltpu.VMEM)
SCALE_IN = INPUT_WIDTH ** (-0.5)
SCALE_RANK = ADAPTER_RANK ** (-0.5)

FIRST = tuple(4 * z + x for x in (2, 3, 1, 0) for z in (5, 6, 4, 7, 3, 2, 1, 0))
LAST = tuple(4 * z + x for z in (5, 6, 4, 7, 3, 2, 1, 0) for x in (2, 3, 1, 0))
ALONG_TENSOR = (4, 5, 6, 3, 7, 2, 1, 0)


def moment_optimizer_step(weights, grads, moment, second):
    fresh_moment = beta_one * moment + (1.0 - beta_one) * grads
    fresh_second = beta_two * second + (1.0 - beta_two) * grads * grads
    first_fix = 1.0 - beta_one**step_number
    second_fix = 1.0 - beta_two**step_number
    return weights - learn_rate * (fresh_moment / first_fix) / (
        jnp.sqrt(fresh_second / second_fix) + adam_eps
    )


def pack_kernel(down_hbm, up_hbm, out_ref, down_ref, up_ref, sems):
    loads = [
        pltpu.make_async_copy(down_hbm, down_ref, sems.at[0]),
        pltpu.make_async_copy(up_hbm, up_ref, sems.at[1]),
    ]
    for load in loads:
        load.start()
    for load in loads:
        load.wait()
    down = down_ref[...].astype(BF16)
    up = up_ref[...]
    rows = jnp.concatenate(
        [down[0], down[1], up[0].T.astype(BF16), up[1].T.astype(BF16)], axis=1
    )
    out_ref[...] = jnp.broadcast_to(rows[None], out_ref.shape)


def turn_kernel(away, x_hbm, d_hbm, out_ref, x_ref, d_ref, sems):
    core = lax.axis_index("node") % 2
    pairs, depth, _ = out_ref.shape
    loads = [
        pltpu.make_async_copy(x_hbm, x_ref, sems.at[0]),
        pltpu.make_async_copy(d_hbm, d_ref, sems.at[1]),
    ]
    for load in loads:
        load.start()
    for spot, piece_ref in enumerate((x_ref, d_ref)):
        loads[spot].wait()
        span = slice(128 * spot, 128 * spot + 128)
        tall = piece_ref[...].T.reshape(pairs, 2, depth, 128)
        for spot, pair in enumerate(FIRST):
            out_ref[spot, :, span] = jnp.where(core == away, tall[pair, 0], tall[pair, 1])


def products(table_ref, tile_ref):
    rows = tile_ref.shape[0] * tile_ref.shape[1]
    wide = lax.dot_general(
        table_ref[...].reshape(rows, 128),
        tile_ref[...].reshape(rows, 256),
        (((0,), (0,)), ((), ())),
        preferred_element_type=F32,
    )
    return jnp.concatenate([wide[0:64, 0:128], wide[64:128, 128:256]], axis=0)


def near_kernel(ids_ref, table_ref, own_ref, other_ref, out_ref):
    out_ref[0:128, 0:128] = products(table_ref, own_ref)
    out_ref[0:128, 128:256] = products(table_ref, other_ref)
    out_ref[128:136] = jnp.broadcast_to(ids_ref[:, 0:1].astype(F32), (8, 256))


def partial_kernel(own_ref, other_ref, out_ref):
    tiles = (
        (own_ref[128:129, 0:128], own_ref[0:128, 0:128] + other_ref[0:128, 128:256]),
        (other_ref[128:129, 0:128], own_ref[0:128, 128:256] + other_ref[0:128, 0:128]),
    )
    parts = []
    for ids, both in tiles:
        first = ids == 0
        parts.append(jnp.where(first, both[0:32], both[32:64]))
        parts.append(jnp.where(first, both[64:96], both[96:128]))
    sums = jnp.concatenate(parts, axis=0).astype(BF16)
    out_ref[...] = jnp.broadcast_to(sums[None], out_ref.shape)


def full_sums(total):
    low = (total[0:32] * SCALE_IN).astype(BF16).astype(F32)
    back = (total[32:64] * SCALE_RANK).astype(BF16).astype(F32)
    return low, back


def by_adapter(ids, values):
    none = jnp.zeros_like(values)
    first = ids == 0
    return [jnp.where(first, values, none), jnp.where(first, none, values)]


def gradient_kernel(own_ids_ref, other_ids_ref, sums_ref, own_ref, other_ref, out_ref):
    total = jnp.sum(sums_ref[...].astype(F32), axis=0)
    pairs, depth, width = own_ref.shape
    grads = jnp.zeros((pairs * depth, 128), F32)
    tiles = ((own_ids_ref, own_ref), (other_ids_ref, other_ref))
    for spot, (ids_ref, tile_ref) in enumerate(tiles):
        ids = ids_ref[128:129, 0:128]
        low, back = full_sums(total[64 * spot : 64 * spot + 64])
        none = [jnp.zeros_like(low)] * 2
        from_x = jnp.concatenate(by_adapter(ids, back) + none, axis=0)
        from_d = jnp.concatenate(none + by_adapter(ids, low), axis=0)
        grads = grads + lax.dot_general(
            tile_ref[...].reshape(pairs * depth, width),
            jnp.concatenate([from_x, from_d], axis=1).astype(BF16),
            (((1,), (1,)), ((), ())),
            preferred_element_type=F32,
        )
    lane = lax.broadcasted_iota(jnp.int32, (1, 128), 1)
    grads = grads * jnp.where(lane < 64, SCALE_IN, SCALE_RANK)
    grads = grads.astype(BF16).reshape(out_ref.shape)
    for spot, pair in enumerate(LAST):
        out_ref[spot] = grads[FIRST.index(pair)]


def grad_input_kernel(ids_ref, sums_ref, own_ref, other_ref, out_ref, table_ref):
    core = lax.axis_index("node") % 2
    for spot, pair in enumerate(FIRST):
        table_ref[pair, core] = own_ref[spot]
        table_ref[pair, 1 - core] = other_ref[spot]
    total = jnp.sum(sums_ref[:, 0:64, :].astype(F32), axis=0)
    _, back = full_sums(total)
    none = [jnp.zeros_like(back)] * 2
    placed = jnp.concatenate(by_adapter(ids_ref[...], back) + none, axis=0)
    table = table_ref[...].reshape(out_ref.shape[1], 128)
    grad = lax.dot_general(
        placed.T.astype(BF16), table, (((1,), (1,)), ((), ())), preferred_element_type=F32
    )
    out_ref[...] = (grad * SCALE_IN).astype(BF16)


def update_kernel(
    terms_ref, wd_ref, wu_ref, md_ref, vd_ref, mu_ref, vu_ref, down_ref, up_ref
):
    total = jnp.sum(terms_ref[...].astype(F32), axis=0)
    for adapter in range(wd_ref.shape[0]):
        grad_a = total[:, 32 * adapter : 32 * adapter + 32]
        grad_b = total[:, 64 + 32 * adapter : 96 + 32 * adapter].T
        down_ref[adapter] = moment_optimizer_step(
            wd_ref[adapter], grad_a, md_ref[adapter], vd_ref[adapter]
        )
        up_ref[adapter] = moment_optimizer_step(
            wu_ref[adapter], grad_b, mu_ref[adapter], vu_ref[adapter]
        )


def call(kernel, out_shape, *args, scratch=()):
    many = isinstance(out_shape, tuple)
    return pl.pallas_call(
        kernel,
        out_shape=out_shape,
        in_specs=[VMEM] * len(args),
        out_specs=(VMEM,) * len(out_shape) if many else VMEM,
        scratch_shapes=scratch,
        compiler_params=pltpu.CompilerParams(vmem_limit_bytes=16 * 2**20),
    )(*args)


def shape(dims, dtype):
    return jax.ShapeDtypeStruct(dims, dtype)


def exchange(blocks, axis, groups=None):
    return lax.all_to_all(
        blocks, axis, split_axis=0, concat_axis=0, axis_index_groups=groups, tiled=True
    )


def local(
    inputs,
    upstream,
    token_adapter_index,
    down_matrices,
    up_matrices,
    down_first_moment,
    down_second_moment,
    up_first_moment,
    up_second_moment,
):
    nodes = lax.axis_size("node")
    shards = lax.axis_size("tensor")
    depth = down_matrices.shape[1]
    pairs = nodes // 2
    first = [[2 * pair + core for pair in FIRST] for core in range(2)]
    last = [[2 * pair + core for pair in LAST] for core in range(2)]

    def swap(block):
        return lax.ppermute(block, "node", [(node, node ^ 1) for node in range(nodes)])

    ids = token_adapter_index.reshape(1, 128)
    packed = pl.pallas_call(
        pack_kernel,
        out_shape=pltpu.VMEM((pairs, depth, 128), BF16),
        in_specs=[pl.BlockSpec(memory_space=pl.ANY)] * 2,
        out_specs=VMEM,
        scratch_shapes=[
            pltpu.VMEM(down_matrices.shape, F32),
            pltpu.VMEM(up_matrices.shape, F32),
            pltpu.SemaphoreType.DMA((2,)),
        ],
        compiler_params=pltpu.CompilerParams(vmem_limit_bytes=16 * 2**20),
    )(
        pltpu.with_memory_space_constraint(down_matrices, pltpu.HBM),
        pltpu.with_memory_space_constraint(up_matrices, pltpu.HBM),
    )
    own = exchange(packed, "node", first)
    rows, width = inputs.shape
    half = shape((pairs, depth, 2 * rows), BF16)
    whole = pltpu.VMEM(inputs.shape, BF16)

    def turn(away, flops):
        return pl.pallas_call(
            functools.partial(turn_kernel, away),
            out_shape=half,
            in_specs=[pl.BlockSpec(memory_space=pl.ANY)] * 2,
            out_specs=VMEM,
            scratch_shapes=[whole, whole, pltpu.SemaphoreType.DMA((2,))],
            compiler_params=pltpu.CompilerParams(vmem_limit_bytes=16 * 2**20),
            cost_estimate=pl.CostEstimate(
                flops=flops, bytes_accessed=2**20, transcendentals=0
            ),
        )(
            pltpu.with_memory_space_constraint(inputs, pltpu.HBM),
            pltpu.with_memory_space_constraint(upstream, pltpu.HBM),
        )

    near = turn(0, 10**10)
    far = turn(1, 0)
    beside = swap(far)
    halves = call(near_kernel, shape((136, 2 * rows), F32), ids, own, near, beside)
    others = swap(halves)
    parts = call(partial_kernel, shape((shards, 128, 128), BF16), halves, others)
    sums = exchange(parts, "tensor", [list(ALONG_TENSOR)])
    other = swap(own)
    terms = call(
        gradient_kernel,
        shape((pairs, depth, 128), BF16),
        halves,
        others,
        sums,
        near,
        beside,
    )
    terms = exchange(terms, "node", last)
    grad_in = call(
        grad_input_kernel,
        shape(inputs.shape, BF16),
        ids,
        sums,
        own,
        other,
        scratch=[pltpu.VMEM((pairs, 2, depth, 128), BF16)],
    )
    down, up = call(
        update_kernel,
        (shape(down_matrices.shape, F32), shape(up_matrices.shape, F32)),
        terms,
        down_matrices,
        up_matrices,
        down_first_moment,
        down_second_moment,
        up_first_moment,
        up_second_moment,
    )
    return (grad_in, down, up)


def solution(mesh):
    return jax.shard_map(
        local,
        mesh=mesh,
        in_specs=(
            P("node", "tensor"),
            P("node", "tensor"),
            P("node"),
            P(None, ("tensor", "node"), None),
            P(None, None, ("tensor", "node")),
            P(None, ("tensor", "node"), None),
            P(None, ("tensor", "node"), None),
            P(None, None, ("tensor", "node")),
            P(None, None, ("tensor", "node")),
        ),
        out_specs=(
            P("node", "tensor"),
            P(None, ("tensor", "node"), None),
            P(None, None, ("tensor", "node")),
        ),
        check_vma=False,
    )
```

```python
import functools

import jax
import jax.numpy as jnp
from jax import lax
from jax.experimental import pallas as pl
from jax.experimental.pallas import tpu as pltpu
from jax.sharding import PartitionSpec as P

INPUT_WIDTH = 16384
ADAPTER_RANK = 32

beta_one = 0.9
beta_two = 0.95
learn_rate = 0.3
adam_eps = 1e-08
step_number = 10

F32 = jnp.float32
BF16 = jnp.bfloat16
VMEM = pl.BlockSpec(memory_space=pltpu.VMEM)
SCALE_IN = INPUT_WIDTH ** (-0.5)
SCALE_RANK = ADAPTER_RANK ** (-0.5)

_AROUND = tuple(4 * z + x for z in range(8) for x in (0, 1, 3, 2))
FIRST = LAST = (22,) + tuple(chip for chip in _AROUND if chip != 22)
ALONG_TENSOR = (4, 5, 6, 3, 7, 2, 1, 0)


def moment_optimizer_step(weights, grads, moment, second):
    fresh_moment = beta_one * moment + (1.0 - beta_one) * grads
    fresh_second = beta_two * second + (1.0 - beta_two) * grads * grads
    first_fix = 1.0 - beta_one**step_number
    second_fix = 1.0 - beta_two**step_number
    return weights - learn_rate * (fresh_moment / first_fix) / (
        jnp.sqrt(fresh_second / second_fix) + adam_eps
    )


def pack_kernel(down_hbm, up_hbm, out_ref, down_ref, up_ref, sems):
    loads = [
        pltpu.make_async_copy(down_hbm, down_ref, sems.at[0]),
        pltpu.make_async_copy(up_hbm, up_ref, sems.at[1]),
    ]
    for load in loads:
        load.start()
    for load in loads:
        load.wait()
    down = down_ref[...].astype(BF16)
    up = up_ref[...]
    rows = jnp.concatenate(
        [down[0], down[1], up[0].T.astype(BF16), up[1].T.astype(BF16)], axis=1
    )
    out_ref[...] = jnp.broadcast_to(rows[None], out_ref.shape)


def turn_kernel(away, x_hbm, d_hbm, out_ref, x_ref, d_ref, sems):
    core = lax.axis_index("node") % 2
    pairs, depth, _ = out_ref.shape
    loads = [
        pltpu.make_async_copy(x_hbm, x_ref, sems.at[0]),
        pltpu.make_async_copy(d_hbm, d_ref, sems.at[1]),
    ]
    for load in loads:
        load.start()
    for spot, piece_ref in enumerate((x_ref, d_ref)):
        loads[spot].wait()
        span = slice(128 * spot, 128 * spot + 128)
        tall = piece_ref[...].T.reshape(pairs, 2, depth, 128)
        for spot, pair in enumerate(FIRST):
            out_ref[spot, :, span] = jnp.where(core == away, tall[pair, 0], tall[pair, 1])


def products(table_ref, tile_ref):
    rows = tile_ref.shape[0] * tile_ref.shape[1]
    wide = lax.dot_general(
        table_ref[...].reshape(rows, 128),
        tile_ref[...].reshape(rows, 256),
        (((0,), (0,)), ((), ())),
        preferred_element_type=F32,
    )
    return jnp.concatenate([wide[0:64, 0:128], wide[64:128, 128:256]], axis=0)


def near_kernel(ids_ref, table_ref, own_ref, other_ref, out_ref):
    out_ref[0:128, 0:128] = products(table_ref, own_ref)
    out_ref[0:128, 128:256] = products(table_ref, other_ref)
    out_ref[128:136] = jnp.broadcast_to(ids_ref[:, 0:1].astype(F32), (8, 256))


def partial_kernel(own_ref, other_ref, out_ref):
    tiles = (
        (own_ref[128:129, 0:128], own_ref[0:128, 0:128] + other_ref[0:128, 128:256]),
        (other_ref[128:129, 0:128], own_ref[0:128, 128:256] + other_ref[0:128, 0:128]),
    )
    parts = []
    for ids, both in tiles:
        first = ids == 0
        parts.append(jnp.where(first, both[0:32], both[32:64]))
        parts.append(jnp.where(first, both[64:96], both[96:128]))
    sums = jnp.concatenate(parts, axis=0).astype(BF16)
    out_ref[...] = jnp.broadcast_to(sums[None], out_ref.shape)


def full_sums(total):
    low = (total[0:32] * SCALE_IN).astype(BF16).astype(F32)
    back = (total[32:64] * SCALE_RANK).astype(BF16).astype(F32)
    return low, back


def by_adapter(ids, values):
    none = jnp.zeros_like(values)
    first = ids == 0
    return [jnp.where(first, values, none), jnp.where(first, none, values)]


def gradient_kernel(own_ids_ref, other_ids_ref, sums_ref, own_ref, other_ref, out_ref):
    total = jnp.sum(sums_ref[...].astype(F32), axis=0)
    pairs, depth, width = own_ref.shape
    grads = jnp.zeros((pairs * depth, 128), F32)
    tiles = ((own_ids_ref, own_ref), (other_ids_ref, other_ref))
    for spot, (ids_ref, tile_ref) in enumerate(tiles):
        ids = ids_ref[128:129, 0:128]
        low, back = full_sums(total[64 * spot : 64 * spot + 64])
        none = [jnp.zeros_like(low)] * 2
        from_x = jnp.concatenate(by_adapter(ids, back) + none, axis=0)
        from_d = jnp.concatenate(none + by_adapter(ids, low), axis=0)
        grads = grads + lax.dot_general(
            tile_ref[...].reshape(pairs * depth, width),
            jnp.concatenate([from_x, from_d], axis=1).astype(BF16),
            (((1,), (1,)), ((), ())),
            preferred_element_type=F32,
        )
    lane = lax.broadcasted_iota(jnp.int32, (1, 128), 1)
    grads = grads * jnp.where(lane < 64, SCALE_IN, SCALE_RANK)
    grads = grads.astype(BF16).reshape(out_ref.shape)
    for spot, pair in enumerate(LAST):
        out_ref[spot] = grads[FIRST.index(pair)]


def grad_input_kernel(ids_ref, sums_ref, own_ref, other_ref, out_ref, table_ref):
    core = lax.axis_index("node") % 2
    for spot, pair in enumerate(FIRST):
        table_ref[pair, core] = own_ref[spot]
        table_ref[pair, 1 - core] = other_ref[spot]
    total = jnp.sum(sums_ref[:, 0:64, :].astype(F32), axis=0)
    _, back = full_sums(total)
    none = [jnp.zeros_like(back)] * 2
    placed = jnp.concatenate(by_adapter(ids_ref[...], back) + none, axis=0)
    table = table_ref[...].reshape(out_ref.shape[1], 128)
    grad = lax.dot_general(
        placed.T.astype(BF16), table, (((1,), (1,)), ((), ())), preferred_element_type=F32
    )
    out_ref[...] = (grad * SCALE_IN).astype(BF16)


def update_kernel(
    terms_ref, wd_ref, wu_ref, md_ref, vd_ref, mu_ref, vu_ref, down_ref, up_ref
):
    total = jnp.sum(terms_ref[...].astype(F32), axis=0)
    for adapter in range(wd_ref.shape[0]):
        grad_a = total[:, 32 * adapter : 32 * adapter + 32]
        grad_b = total[:, 64 + 32 * adapter : 96 + 32 * adapter].T
        down_ref[adapter] = moment_optimizer_step(
            wd_ref[adapter], grad_a, md_ref[adapter], vd_ref[adapter]
        )
        up_ref[adapter] = moment_optimizer_step(
            wu_ref[adapter], grad_b, mu_ref[adapter], vu_ref[adapter]
        )


def call(kernel, out_shape, *args, scratch=()):
    many = isinstance(out_shape, tuple)
    return pl.pallas_call(
        kernel,
        out_shape=out_shape,
        in_specs=[VMEM] * len(args),
        out_specs=(VMEM,) * len(out_shape) if many else VMEM,
        scratch_shapes=scratch,
        compiler_params=pltpu.CompilerParams(vmem_limit_bytes=16 * 2**20),
    )(*args)


def shape(dims, dtype):
    return jax.ShapeDtypeStruct(dims, dtype)


def exchange(blocks, axis, groups=None):
    return lax.all_to_all(
        blocks, axis, split_axis=0, concat_axis=0, axis_index_groups=groups, tiled=True
    )


def local(
    inputs,
    upstream,
    token_adapter_index,
    down_matrices,
    up_matrices,
    down_first_moment,
    down_second_moment,
    up_first_moment,
    up_second_moment,
):
    nodes = lax.axis_size("node")
    shards = lax.axis_size("tensor")
    depth = down_matrices.shape[1]
    pairs = nodes // 2
    first = [[2 * pair + core for pair in FIRST] for core in range(2)]
    last = [[2 * pair + core for pair in LAST] for core in range(2)]

    def swap(block):
        return lax.ppermute(block, "node", [(node, node ^ 1) for node in range(nodes)])

    ids = token_adapter_index.reshape(1, 128)
    packed = pl.pallas_call(
        pack_kernel,
        out_shape=pltpu.VMEM((pairs, depth, 128), BF16),
        in_specs=[pl.BlockSpec(memory_space=pl.ANY)] * 2,
        out_specs=VMEM,
        scratch_shapes=[
            pltpu.VMEM(down_matrices.shape, F32),
            pltpu.VMEM(up_matrices.shape, F32),
            pltpu.SemaphoreType.DMA((2,)),
        ],
        compiler_params=pltpu.CompilerParams(vmem_limit_bytes=16 * 2**20),
    )(
        pltpu.with_memory_space_constraint(down_matrices, pltpu.HBM),
        pltpu.with_memory_space_constraint(up_matrices, pltpu.HBM),
    )
    own = exchange(packed, "node", first)
    rows, width = inputs.shape
    half = shape((pairs, depth, 2 * rows), BF16)
    whole = pltpu.VMEM(inputs.shape, BF16)

    def turn(away, flops):
        return pl.pallas_call(
            functools.partial(turn_kernel, away),
            out_shape=half,
            in_specs=[pl.BlockSpec(memory_space=pl.ANY)] * 2,
            out_specs=VMEM,
            scratch_shapes=[whole, whole, pltpu.SemaphoreType.DMA((2,))],
            compiler_params=pltpu.CompilerParams(vmem_limit_bytes=16 * 2**20),
            cost_estimate=pl.CostEstimate(
                flops=flops, bytes_accessed=2**20, transcendentals=0
            ),
        )(
            pltpu.with_memory_space_constraint(inputs, pltpu.HBM),
            pltpu.with_memory_space_constraint(upstream, pltpu.HBM),
        )

    near = turn(0, 10**10)
    far = turn(1, 0)
    beside = swap(far)
    halves = call(near_kernel, shape((136, 2 * rows), F32), ids, own, near, beside)
    others = swap(halves)
    parts = call(partial_kernel, shape((shards, 128, 128), BF16), halves, others)
    sums = exchange(parts, "tensor", [list(ALONG_TENSOR)])
    other = swap(own)
    terms = call(
        gradient_kernel,
        shape((pairs, depth, 128), BF16),
        halves,
        others,
        sums,
        near,
        beside,
    )
    terms = exchange(terms, "node", last)
    grad_in = call(
        grad_input_kernel,
        shape(inputs.shape, BF16),
        ids,
        sums,
        own,
        other,
        scratch=[pltpu.VMEM((pairs, 2, depth, 128), BF16)],
    )
    down, up = call(
        update_kernel,
        (shape(down_matrices.shape, F32), shape(up_matrices.shape, F32)),
        terms,
        down_matrices,
        up_matrices,
        down_first_moment,
        down_second_moment,
        up_first_moment,
        up_second_moment,
    )
    return (grad_in, down, up)


def solution(mesh):
    return jax.shard_map(
        local,
        mesh=mesh,
        in_specs=(
            P("node", "tensor"),
            P("node", "tensor"),
            P("node"),
            P(None, ("tensor", "node"), None),
            P(None, None, ("tensor", "node")),
            P(None, ("tensor", "node"), None),
            P(None, ("tensor", "node"), None),
            P(None, None, ("tensor", "node")),
            P(None, None, ("tensor", "node")),
        ),
        out_specs=(
            P("node", "tensor"),
            P(None, ("tensor", "node"), None),
            P(None, None, ("tensor", "node")),
        ),
        check_vma=False,
    )
```

```python
import functools

import jax
import jax.numpy as jnp
from jax import lax
from jax.experimental import pallas as pl
from jax.experimental.pallas import tpu as pltpu
from jax.sharding import PartitionSpec as P

INPUT_WIDTH = 16384
ADAPTER_RANK = 32

beta_one = 0.9
beta_two = 0.95
learn_rate = 0.3
adam_eps = 1e-08
step_number = 10

F32 = jnp.float32
BF16 = jnp.bfloat16
VMEM = pl.BlockSpec(memory_space=pltpu.VMEM)
SCALE_IN = INPUT_WIDTH ** (-0.5)
SCALE_RANK = ADAPTER_RANK ** (-0.5)

_AROUND = tuple(4 * z + x for z in range(8) for x in (0, 1, 3, 2))
CHIPS = (22,) + tuple(chip for chip in _AROUND if chip != 22)
NODES = tuple(2 * chip + core for chip in CHIPS for core in range(2))
LAST_CHIPS = (18,) + tuple(chip for chip in _AROUND if chip != 18)
LAST_NODES = tuple(2 * chip + core for chip in LAST_CHIPS for core in range(2))
ALONG_TENSOR = (4, 5, 6, 3, 7, 2, 1, 0)
NEAR_FLOPS = 10**10


def moment_optimizer_step(weights, grads, moment, second):
    fresh_moment = beta_one * moment + (1.0 - beta_one) * grads
    fresh_second = beta_two * second + (1.0 - beta_two) * grads * grads
    first_fix = 1.0 - beta_one**step_number
    second_fix = 1.0 - beta_two**step_number
    return weights - learn_rate * (fresh_moment / first_fix) / (
        jnp.sqrt(fresh_second / second_fix) + adam_eps
    )


def folded(rows):
    half = rows.shape[0] // 2
    return jnp.concatenate([rows[:half], rows[half:]], axis=1)


def pack_kernel(down_hbm, up_hbm, out_ref, down_ref, up_ref, sems):
    loads = [
        pltpu.make_async_copy(down_hbm, down_ref, sems.at[0]),
        pltpu.make_async_copy(up_hbm, up_ref, sems.at[1]),
    ]
    for load in loads:
        load.start()
    for load in loads:
        load.wait()
    down = down_ref[...].astype(BF16)
    up = up_ref[...]
    both = [
        folded(jnp.concatenate([down[0], down[1]], axis=1)),
        folded(jnp.concatenate([up[0].T, up[1].T], axis=1).astype(BF16)),
    ]
    for spot, node in enumerate(NODES):
        out_ref[spot] = both[node % 2]


def away_kernel(second, ids_hbm, x_hbm, d_hbm, out_ref, piece_ref, ids_ref, sems):
    core = lax.axis_index("node") % 2
    inputs_next = core == 1 - second
    load_ids = pltpu.make_async_copy(ids_hbm, ids_ref, sems.at[1])
    load_ids.start()

    @pl.when(inputs_next)
    def _():
        load = pltpu.make_async_copy(x_hbm, piece_ref, sems.at[0])
        load.start()
        load.wait()

    @pl.when(jnp.logical_not(inputs_next))
    def _():
        load = pltpu.make_async_copy(d_hbm, piece_ref, sems.at[0])
        load.start()
        load.wait()

    load_ids.wait()
    turned = piece_ref[...].T.reshape(len(NODES), -1, 128)
    for spot, node in enumerate(NODES):
        out_ref[spot] = turned[node]
    if not second:
        mark = jnp.broadcast_to(ids_ref[:, 0:1].astype(F32), out_ref.shape[1:])
        out_ref[len(NODES)] = mark.astype(BF16)


def mine_kernel(x_hbm, d_hbm, out_ref, x_ref, d_ref, sems):
    core = lax.axis_index("node") % 2
    loads = [
        pltpu.make_async_copy(x_hbm, x_ref, sems.at[0]),
        pltpu.make_async_copy(d_hbm, d_ref, sems.at[1]),
    ]
    for load in loads:
        load.start()
    turned = []
    for load, piece_ref in zip(loads, (x_ref, d_ref)):
        load.wait()
        turned.append(piece_ref[...].T.reshape(len(NODES), -1, 128))
    for spot, node in enumerate(NODES):
        x, d = turned[0][node], turned[1][node]
        out_ref[spot, :, 0:128] = jnp.where(core == 0, x, d)
        out_ref[spot, :, 128:256] = jnp.where(core == 0, d, x)


def other_ids(beside_ref):
    return beside_ref[len(NODES), 0:16, :].astype(F32)[0:1]


def partial_kernel(ids_ref, table_ref, mine_ref, beside_ref, out_ref):
    count, half, _ = table_ref.shape
    table = table_ref[...].reshape(count * half, 128)
    parts = []
    for ids, tile_ref in ((ids_ref[...].astype(F32), mine_ref), (other_ids(beside_ref), beside_ref)):
        both = jnp.zeros((64, 128), F32)
        for side in range(2):
            features = tile_ref[0:count, half * side : half * side + half, 0:128]
            wide = lax.dot_general(
                table,
                features.reshape(count * half, 128),
                (((0,), (0,)), ((), ())),
                preferred_element_type=F32,
            )
            both = both + wide[64 * side : 64 * side + 64]
        parts.append(jnp.where(ids == 0, both[0:32], both[32:64]))
    sums = jnp.concatenate(parts, axis=0).astype(BF16)
    out_ref[...] = jnp.broadcast_to(sums[None], out_ref.shape)


def by_adapter(ids, values):
    none = jnp.zeros_like(values)
    first = ids == 0
    return [jnp.where(first, values, none), jnp.where(first, none, values)]


def gradient_kernel(ids_ref, sums_ref, marked_ref, mine_ref, beside_ref, out_ref):
    core = lax.axis_index("node") % 2
    total = jnp.sum(sums_ref[...].astype(F32), axis=0)
    total = (total * jnp.where(core == 0, SCALE_IN, SCALE_RANK)).astype(BF16).astype(F32)
    count, half, _ = out_ref.shape
    grads = jnp.zeros((count * 2 * half, 128), F32)
    tiles = (
        (ids_ref[...].astype(F32), mine_ref[:, :, 128:256]),
        (other_ids(marked_ref), beside_ref[...]),
    )
    for spot, (ids, tile) in enumerate(tiles):
        halves = by_adapter(ids, total[32 * spot : 32 * spot + 32])
        grads = grads + lax.dot_general(
            tile.reshape(count * 2 * half, 128),
            jnp.concatenate(halves * 2, axis=0).astype(BF16),
            (((1,), (1,)), ((), ())),
            preferred_element_type=F32,
        )
    grads = grads * jnp.where(core == 0, SCALE_RANK, SCALE_IN)
    grads = grads.reshape(count, 2, half, 128)
    lane = lax.broadcasted_iota(jnp.int32, (1, 1, 128), 2)
    grads = jnp.where(lane < 64, grads[:, 0], grads[:, 1]).astype(BF16)
    for spot, node in enumerate(LAST_NODES):
        out_ref[spot] = grads[NODES.index(node)]


def grad_input_kernel(ids_ref, sums_ref, other_sums_ref, own_ref, other_ref, out_ref, table_ref):
    core = lax.axis_index("node") % 2
    lane = lax.broadcasted_iota(jnp.int32, (1, 128), 1)
    for spot, node in enumerate(NODES):
        block = jnp.where(core == 0, own_ref[spot], other_ref[spot])
        none = jnp.zeros_like(block)
        table_ref[node, 0] = jnp.where(lane < 64, block, none)
        table_ref[node, 1] = jnp.where(lane < 64, none, block)
    terms = jnp.where(core == 0, other_sums_ref[:, 32:64, :], sums_ref[:, 0:32, :])
    total = jnp.sum(terms.astype(F32), axis=0)
    back = (total * SCALE_RANK).astype(BF16).astype(F32)
    placed = jnp.concatenate(by_adapter(ids_ref[...], back) * 2, axis=0)
    table = table_ref[...].reshape(out_ref.shape[1], 128)
    grad = lax.dot_general(
        placed.T.astype(BF16), table, (((1,), (1,)), ((), ())), preferred_element_type=F32
    )
    out_ref[...] = (grad * SCALE_IN).astype(BF16)


def update_kernel(
    terms_ref, wd_ref, wu_ref, md_ref, vd_ref, mu_ref, vu_ref, down_ref, up_ref
):
    terms = terms_ref[...].astype(F32)
    terms = terms.reshape(terms.shape[0] // 2, 2, *terms.shape[1:])
    total = jnp.sum(terms, axis=0)
    sums = [jnp.concatenate([both[:, 0:64], both[:, 64:128]], axis=0) for both in total]
    for adapter in range(wd_ref.shape[0]):
        grad_a = sums[1][:, 32 * adapter : 32 * adapter + 32]
        grad_b = sums[0][:, 32 * adapter : 32 * adapter + 32].T
        down_ref[adapter] = moment_optimizer_step(
            wd_ref[adapter], grad_a, md_ref[adapter], vd_ref[adapter]
        )
        up_ref[adapter] = moment_optimizer_step(
            wu_ref[adapter], grad_b, mu_ref[adapter], vu_ref[adapter]
        )


def call(kernel, out_shape, *args, scratch=()):
    many = isinstance(out_shape, tuple)
    return pl.pallas_call(
        kernel,
        out_shape=out_shape,
        in_specs=[VMEM] * len(args),
        out_specs=(VMEM,) * len(out_shape) if many else VMEM,
        scratch_shapes=scratch,
        compiler_params=pltpu.CompilerParams(vmem_limit_bytes=16 * 2**20),
    )(*args)


def shape(dims, dtype):
    return jax.ShapeDtypeStruct(dims, dtype)


def exchange(blocks, axis, groups=None):
    return lax.all_to_all(
        blocks, axis, split_axis=0, concat_axis=0, axis_index_groups=groups, tiled=True
    )


def local(
    inputs,
    upstream,
    token_adapter_index,
    down_matrices,
    up_matrices,
    down_first_moment,
    down_second_moment,
    up_first_moment,
    up_second_moment,
):
    nodes = lax.axis_size("node")
    shards = lax.axis_size("tensor")
    depth = down_matrices.shape[1]
    def swap(block):
        return lax.ppermute(block, "node", [(node, node ^ 1) for node in range(nodes)])

    ids = token_adapter_index.reshape(1, 128)
    packed = pl.pallas_call(
        pack_kernel,
        out_shape=shape((nodes, depth // 2, 128), BF16),
        in_specs=[pl.BlockSpec(memory_space=pl.ANY)] * 2,
        out_specs=VMEM,
        scratch_shapes=[
            pltpu.VMEM(down_matrices.shape, F32),
            pltpu.VMEM(up_matrices.shape, F32),
            pltpu.SemaphoreType.DMA((2,)),
        ],
        compiler_params=pltpu.CompilerParams(vmem_limit_bytes=16 * 2**20),
    )(
        pltpu.with_memory_space_constraint(down_matrices, pltpu.HBM),
        pltpu.with_memory_space_constraint(up_matrices, pltpu.HBM),
    )
    own = exchange(packed, "node", [list(NODES)])
    rows = inputs.shape[0]
    whole = pltpu.VMEM(inputs.shape, BF16)

    def turn(kernel, dims, scratch, *small, flops=0):
        return pl.pallas_call(
            kernel,
            out_shape=shape(dims, BF16),
            in_specs=[pl.BlockSpec(memory_space=pl.ANY)] * (len(small) + 2),
            out_specs=VMEM,
            scratch_shapes=[*scratch, pltpu.SemaphoreType.DMA((2,))],
            compiler_params=pltpu.CompilerParams(vmem_limit_bytes=16 * 2**20),
            cost_estimate=pl.CostEstimate(
                flops=flops, bytes_accessed=2**20, transcendentals=0
            ),
        )(
            *(pltpu.with_memory_space_constraint(one, pltpu.HBM) for one in small),
            pltpu.with_memory_space_constraint(inputs, pltpu.HBM),
            pltpu.with_memory_space_constraint(upstream, pltpu.HBM),
        )

    def away(second):
        dims = (nodes + 1 - second, depth, rows)
        scratch = [whole, pltpu.VMEM(ids.shape, jnp.int32)]
        return swap(turn(functools.partial(away_kernel, second), dims, scratch, ids))

    beside, rest = away(0), away(1)
    mine = turn(mine_kernel, (nodes, depth, 2 * rows), [whole, whole], flops=NEAR_FLOPS)
    own, mine = lax.optimization_barrier((own, mine))
    beside, rest = lax.optimization_barrier((beside, rest))
    parts = call(partial_kernel, shape((shards, 64, 128), BF16), ids, own, mine, beside)
    sums = exchange(parts, "tensor", [list(ALONG_TENSOR)])
    other = swap(own)
    terms = call(
        gradient_kernel, shape((nodes, depth // 2, 128), BF16), ids, sums, beside, mine, rest
    )
    terms = exchange(terms, "node", [list(LAST_NODES)])
    grad_in = call(
        grad_input_kernel,
        shape(inputs.shape, BF16),
        ids,
        sums,
        swap(sums),
        own,
        other,
        scratch=[pltpu.VMEM((nodes, 2, depth // 2, 128), BF16)],
    )
    down, up = call(
        update_kernel,
        (shape(down_matrices.shape, F32), shape(up_matrices.shape, F32)),
        terms,
        down_matrices,
        up_matrices,
        down_first_moment,
        down_second_moment,
        up_first_moment,
        up_second_moment,
    )
    return (grad_in, down, up)


def solution(mesh):
    return jax.shard_map(
        local,
        mesh=mesh,
        in_specs=(
            P("node", "tensor"),
            P("node", "tensor"),
            P("node"),
            P(None, ("tensor", "node"), None),
            P(None, None, ("tensor", "node")),
            P(None, ("tensor", "node"), None),
            P(None, ("tensor", "node"), None),
            P(None, None, ("tensor", "node")),
            P(None, None, ("tensor", "node")),
        ),
        out_specs=(
            P("node", "tensor"),
            P(None, ("tensor", "node"), None),
            P(None, None, ("tensor", "node")),
        ),
        check_vma=False,
    )
```

```python
import functools

import jax
import jax.numpy as jnp
from jax import lax
from jax.experimental import pallas as pl
from jax.experimental.pallas import tpu as pltpu
from jax.sharding import PartitionSpec as P

INPUT_WIDTH = 16384
ADAPTER_RANK = 32

beta_one = 0.9
beta_two = 0.95
learn_rate = 0.3
adam_eps = 1e-08
step_number = 10

F32 = jnp.float32
BF16 = jnp.bfloat16
VMEM = pl.BlockSpec(memory_space=pltpu.VMEM)
SCALE_IN = INPUT_WIDTH ** (-0.5)
SCALE_RANK = ADAPTER_RANK ** (-0.5)

_AROUND = tuple(4 * z + x for z in range(8) for x in (0, 1, 3, 2))
CHIPS = (26,) + tuple(chip for chip in _AROUND if chip != 26)
NODES = tuple(2 * chip + core for chip in CHIPS for core in range(2))
LAST_CHIPS = (18,) + tuple(chip for chip in _AROUND if chip != 18)
LAST_NODES = tuple(2 * chip + core for chip in LAST_CHIPS for core in range(2))
ALONG_TENSOR = (4, 5, 6, 3, 7, 2, 1, 0)
NEAR_FLOPS = 10**10


def moment_optimizer_step(weights, grads, moment, second):
    fresh_moment = beta_one * moment + (1.0 - beta_one) * grads
    fresh_second = beta_two * second + (1.0 - beta_two) * grads * grads
    first_fix = 1.0 - beta_one**step_number
    second_fix = 1.0 - beta_two**step_number
    return weights - learn_rate * (fresh_moment / first_fix) / (
        jnp.sqrt(fresh_second / second_fix) + adam_eps
    )


def folded(rows):
    half = rows.shape[0] // 2
    return jnp.concatenate([rows[:half], rows[half:]], axis=1)


def pack_kernel(down_hbm, up_hbm, out_ref, down_ref, up_ref, sems):
    loads = [
        pltpu.make_async_copy(down_hbm, down_ref, sems.at[0]),
        pltpu.make_async_copy(up_hbm, up_ref, sems.at[1]),
    ]
    for load in loads:
        load.start()
    for load in loads:
        load.wait()
    down = down_ref[...].astype(BF16)
    up = up_ref[...]
    both = [
        folded(jnp.concatenate([down[0], down[1]], axis=1)),
        folded(jnp.concatenate([up[0].T, up[1].T], axis=1).astype(BF16)),
    ]
    for spot, node in enumerate(NODES):
        out_ref[spot] = both[node % 2]


def away_kernel(second, ids_hbm, x_hbm, d_hbm, out_ref, piece_ref, ids_ref, sems):
    core = lax.axis_index("node") % 2
    inputs_next = core == 1 - second
    load_ids = pltpu.make_async_copy(ids_hbm, ids_ref, sems.at[1])
    load_ids.start()

    @pl.when(inputs_next)
    def _():
        load = pltpu.make_async_copy(x_hbm, piece_ref, sems.at[0])
        load.start()
        load.wait()

    @pl.when(jnp.logical_not(inputs_next))
    def _():
        load = pltpu.make_async_copy(d_hbm, piece_ref, sems.at[0])
        load.start()
        load.wait()

    load_ids.wait()
    turned = piece_ref[...].T.reshape(len(NODES), -1, 128)
    for spot, node in enumerate(NODES):
        out_ref[spot] = turned[node]
    if not second:
        mark = jnp.broadcast_to(ids_ref[:, 0:1].astype(F32), out_ref.shape[1:])
        out_ref[len(NODES)] = mark.astype(BF16)


def mine_kernel(x_hbm, d_hbm, out_ref, x_ref, d_ref, sems):
    core = lax.axis_index("node") % 2
    loads = [
        pltpu.make_async_copy(x_hbm, x_ref, sems.at[0]),
        pltpu.make_async_copy(d_hbm, d_ref, sems.at[1]),
    ]
    for load in loads:
        load.start()
    turned = []
    for load, piece_ref in zip(loads, (x_ref, d_ref)):
        load.wait()
        turned.append(piece_ref[...].T.reshape(len(NODES), -1, 128))
    for spot, node in enumerate(NODES):
        x, d = turned[0][node], turned[1][node]
        out_ref[spot, :, 0:128] = jnp.where(core == 0, x, d)
        out_ref[spot, :, 128:256] = jnp.where(core == 0, d, x)


def other_ids(beside_ref):
    return beside_ref[len(NODES), 0:16, :].astype(F32)[0:1]


def partial_kernel(ids_ref, table_ref, mine_ref, beside_ref, out_ref):
    count, half, _ = table_ref.shape
    table = table_ref[...].reshape(count * half, 128)
    parts = []
    for ids, tile_ref in ((ids_ref[...].astype(F32), mine_ref), (other_ids(beside_ref), beside_ref)):
        both = jnp.zeros((64, 128), F32)
        for side in range(2):
            features = tile_ref[0:count, half * side : half * side + half, 0:128]
            wide = lax.dot_general(
                table,
                features.reshape(count * half, 128),
                (((0,), (0,)), ((), ())),
                preferred_element_type=F32,
            )
            both = both + wide[64 * side : 64 * side + 64]
        parts.append(jnp.where(ids == 0, both[0:32], both[32:64]))
    sums = jnp.concatenate(parts, axis=0).astype(BF16)
    out_ref[...] = jnp.broadcast_to(sums[None], out_ref.shape)


def by_adapter(ids, values):
    none = jnp.zeros_like(values)
    first = ids == 0
    return [jnp.where(first, values, none), jnp.where(first, none, values)]


def gradient_kernel(ids_ref, sums_ref, marked_ref, mine_ref, beside_ref, out_ref):
    core = lax.axis_index("node") % 2
    total = jnp.sum(sums_ref[...].astype(F32), axis=0)
    total = (total * jnp.where(core == 0, SCALE_IN, SCALE_RANK)).astype(BF16).astype(F32)
    count, half, _ = out_ref.shape
    grads = jnp.zeros((count * 2 * half, 128), F32)
    tiles = (
        (ids_ref[...].astype(F32), mine_ref[:, :, 128:256]),
        (other_ids(marked_ref), beside_ref[...]),
    )
    for spot, (ids, tile) in enumerate(tiles):
        halves = by_adapter(ids, total[32 * spot : 32 * spot + 32])
        grads = grads + lax.dot_general(
            tile.reshape(count * 2 * half, 128),
            jnp.concatenate(halves * 2, axis=0).astype(BF16),
            (((1,), (1,)), ((), ())),
            preferred_element_type=F32,
        )
    grads = grads * jnp.where(core == 0, SCALE_RANK, SCALE_IN)
    grads = grads.reshape(count, 2, half, 128)
    lane = lax.broadcasted_iota(jnp.int32, (1, 1, 128), 2)
    grads = jnp.where(lane < 64, grads[:, 0], grads[:, 1]).astype(BF16)
    for spot, node in enumerate(LAST_NODES):
        out_ref[spot] = grads[NODES.index(node)]


def grad_input_kernel(ids_ref, sums_ref, other_sums_ref, own_ref, other_ref, out_ref, table_ref):
    core = lax.axis_index("node") % 2
    lane = lax.broadcasted_iota(jnp.int32, (1, 128), 1)
    for spot, node in enumerate(NODES):
        block = jnp.where(core == 0, own_ref[spot], other_ref[spot])
        none = jnp.zeros_like(block)
        table_ref[node, 0] = jnp.where(lane < 64, block, none)
        table_ref[node, 1] = jnp.where(lane < 64, none, block)
    terms = jnp.where(core == 0, other_sums_ref[:, 32:64, :], sums_ref[:, 0:32, :])
    total = jnp.sum(terms.astype(F32), axis=0)
    back = (total * SCALE_RANK).astype(BF16).astype(F32)
    placed = jnp.concatenate(by_adapter(ids_ref[...], back) * 2, axis=0)
    table = table_ref[...].reshape(out_ref.shape[1], 128)
    grad = lax.dot_general(
        placed.T.astype(BF16), table, (((1,), (1,)), ((), ())), preferred_element_type=F32
    )
    out_ref[...] = (grad * SCALE_IN).astype(BF16)


def update_kernel(
    terms_ref, wd_ref, wu_ref, md_ref, vd_ref, mu_ref, vu_ref, down_ref, up_ref
):
    terms = terms_ref[...].astype(F32)
    terms = terms.reshape(terms.shape[0] // 2, 2, *terms.shape[1:])
    total = jnp.sum(terms, axis=0)
    sums = [jnp.concatenate([both[:, 0:64], both[:, 64:128]], axis=0) for both in total]
    for adapter in range(wd_ref.shape[0]):
        grad_a = sums[1][:, 32 * adapter : 32 * adapter + 32]
        grad_b = sums[0][:, 32 * adapter : 32 * adapter + 32].T
        down_ref[adapter] = moment_optimizer_step(
            wd_ref[adapter], grad_a, md_ref[adapter], vd_ref[adapter]
        )
        up_ref[adapter] = moment_optimizer_step(
            wu_ref[adapter], grad_b, mu_ref[adapter], vu_ref[adapter]
        )


def call(kernel, out_shape, *args, scratch=()):
    many = isinstance(out_shape, tuple)
    return pl.pallas_call(
        kernel,
        out_shape=out_shape,
        in_specs=[VMEM] * len(args),
        out_specs=(VMEM,) * len(out_shape) if many else VMEM,
        scratch_shapes=scratch,
        compiler_params=pltpu.CompilerParams(vmem_limit_bytes=16 * 2**20),
    )(*args)


def shape(dims, dtype):
    return jax.ShapeDtypeStruct(dims, dtype)


def exchange(blocks, axis, groups=None):
    return lax.all_to_all(
        blocks, axis, split_axis=0, concat_axis=0, axis_index_groups=groups, tiled=True
    )


def local(
    inputs,
    upstream,
    token_adapter_index,
    down_matrices,
    up_matrices,
    down_first_moment,
    down_second_moment,
    up_first_moment,
    up_second_moment,
):
    nodes = lax.axis_size("node")
    shards = lax.axis_size("tensor")
    depth = down_matrices.shape[1]
    def swap(block):
        return lax.ppermute(block, "node", [(node, node ^ 1) for node in range(nodes)])

    ids = token_adapter_index.reshape(1, 128)
    packed = pl.pallas_call(
        pack_kernel,
        out_shape=shape((nodes, depth // 2, 128), BF16),
        in_specs=[pl.BlockSpec(memory_space=pl.ANY)] * 2,
        out_specs=VMEM,
        scratch_shapes=[
            pltpu.VMEM(down_matrices.shape, F32),
            pltpu.VMEM(up_matrices.shape, F32),
            pltpu.SemaphoreType.DMA((2,)),
        ],
        compiler_params=pltpu.CompilerParams(vmem_limit_bytes=16 * 2**20),
    )(
        pltpu.with_memory_space_constraint(down_matrices, pltpu.HBM),
        pltpu.with_memory_space_constraint(up_matrices, pltpu.HBM),
    )
    own = exchange(packed, "node", [list(NODES)])
    rows = inputs.shape[0]
    whole = pltpu.VMEM(inputs.shape, BF16)

    def turn(kernel, dims, scratch, *small, flops=0):
        return pl.pallas_call(
            kernel,
            out_shape=shape(dims, BF16),
            in_specs=[pl.BlockSpec(memory_space=pl.ANY)] * (len(small) + 2),
            out_specs=VMEM,
            scratch_shapes=[*scratch, pltpu.SemaphoreType.DMA((2,))],
            compiler_params=pltpu.CompilerParams(vmem_limit_bytes=16 * 2**20),
            cost_estimate=pl.CostEstimate(
                flops=flops, bytes_accessed=2**20, transcendentals=0
            ),
        )(
            *(pltpu.with_memory_space_constraint(one, pltpu.HBM) for one in small),
            pltpu.with_memory_space_constraint(inputs, pltpu.HBM),
            pltpu.with_memory_space_constraint(upstream, pltpu.HBM),
        )

    def away(second):
        dims = (nodes + 1 - second, depth, rows)
        scratch = [whole, pltpu.VMEM(ids.shape, jnp.int32)]
        return swap(turn(functools.partial(away_kernel, second), dims, scratch, ids))

    beside, rest = away(0), away(1)
    mine = turn(mine_kernel, (nodes, depth, 2 * rows), [whole, whole], flops=NEAR_FLOPS)
    own, mine = lax.optimization_barrier((own, mine))
    beside, rest = lax.optimization_barrier((beside, rest))
    parts = call(partial_kernel, shape((shards, 64, 128), BF16), ids, own, mine, beside)
    sums = exchange(parts, "tensor", [list(ALONG_TENSOR)])
    other = swap(own)
    terms = call(
        gradient_kernel, shape((nodes, depth // 2, 128), BF16), ids, sums, beside, mine, rest
    )
    terms = exchange(terms, "node", [list(LAST_NODES)])
    grad_in = call(
        grad_input_kernel,
        shape(inputs.shape, BF16),
        ids,
        sums,
        swap(sums),
        own,
        other,
        scratch=[pltpu.VMEM((nodes, 2, depth // 2, 128), BF16)],
    )
    down, up = call(
        update_kernel,
        (shape(down_matrices.shape, F32), shape(up_matrices.shape, F32)),
        terms,
        down_matrices,
        up_matrices,
        down_first_moment,
        down_second_moment,
        up_first_moment,
        up_second_moment,
    )
    return (grad_in, down, up)


def solution(mesh):
    return jax.shard_map(
        local,
        mesh=mesh,
        in_specs=(
            P("node", "tensor"),
            P("node", "tensor"),
            P("node"),
            P(None, ("tensor", "node"), None),
            P(None, None, ("tensor", "node")),
            P(None, ("tensor", "node"), None),
            P(None, ("tensor", "node"), None),
            P(None, None, ("tensor", "node")),
            P(None, None, ("tensor", "node")),
        ),
        out_specs=(
            P("node", "tensor"),
            P(None, ("tensor", "node"), None),
            P(None, None, ("tensor", "node")),
        ),
        check_vma=False,
    )
```

```python
import functools

import jax
import jax.numpy as jnp
from jax import lax
from jax.experimental import pallas as pl
from jax.experimental.pallas import tpu as pltpu
from jax.sharding import PartitionSpec as P

INPUT_WIDTH = 16384
ADAPTER_RANK = 32

beta_one = 0.9
beta_two = 0.95
learn_rate = 0.3
adam_eps = 1e-08
step_number = 10

F32 = jnp.float32
BF16 = jnp.bfloat16
VMEM = pl.BlockSpec(memory_space=pltpu.VMEM)
SCALE_IN = INPUT_WIDTH ** (-0.5)
SCALE_RANK = ADAPTER_RANK ** (-0.5)

_AROUND = tuple(4 * z + x for z in range(8) for x in (0, 1, 3, 2))
CHIPS = (27,) + tuple(chip for chip in _AROUND if chip != 27)
NODES = tuple(2 * chip + core for chip in CHIPS for core in range(2))
LAST_CHIPS = (18,) + tuple(chip for chip in _AROUND if chip != 18)
LAST_NODES = tuple(2 * chip + core for chip in LAST_CHIPS for core in range(2))
ALONG_TENSOR = (4, 5, 6, 3, 7, 2, 1, 0)
NEAR_FLOPS = 10**10


def moment_optimizer_step(weights, grads, moment, second):
    fresh_moment = beta_one * moment + (1.0 - beta_one) * grads
    fresh_second = beta_two * second + (1.0 - beta_two) * grads * grads
    first_fix = 1.0 - beta_one**step_number
    second_fix = 1.0 - beta_two**step_number
    return weights - learn_rate * (fresh_moment / first_fix) / (
        jnp.sqrt(fresh_second / second_fix) + adam_eps
    )


def folded(rows):
    half = rows.shape[0] // 2
    return jnp.concatenate([rows[:half], rows[half:]], axis=1)


def pack_kernel(down_hbm, up_hbm, out_ref, down_ref, up_ref, sems):
    loads = [
        pltpu.make_async_copy(down_hbm, down_ref, sems.at[0]),
        pltpu.make_async_copy(up_hbm, up_ref, sems.at[1]),
    ]
    for load in loads:
        load.start()
    for load in loads:
        load.wait()
    down = down_ref[...].astype(BF16)
    up = up_ref[...]
    both = [
        folded(jnp.concatenate([down[0], down[1]], axis=1)),
        folded(jnp.concatenate([up[0].T, up[1].T], axis=1).astype(BF16)),
    ]
    for spot, node in enumerate(NODES):
        out_ref[spot] = both[node % 2]


def away_kernel(second, ids_hbm, x_hbm, d_hbm, out_ref, piece_ref, ids_ref, sems):
    core = lax.axis_index("node") % 2
    inputs_next = core == 1 - second
    load_ids = pltpu.make_async_copy(ids_hbm, ids_ref, sems.at[1])
    load_ids.start()

    @pl.when(inputs_next)
    def _():
        load = pltpu.make_async_copy(x_hbm, piece_ref, sems.at[0])
        load.start()
        load.wait()

    @pl.when(jnp.logical_not(inputs_next))
    def _():
        load = pltpu.make_async_copy(d_hbm, piece_ref, sems.at[0])
        load.start()
        load.wait()

    load_ids.wait()
    turned = piece_ref[...].T.reshape(len(NODES), -1, 128)
    for spot, node in enumerate(NODES):
        out_ref[spot] = turned[node]
    if not second:
        mark = jnp.broadcast_to(ids_ref[:, 0:1].astype(F32), out_ref.shape[1:])
        out_ref[len(NODES)] = mark.astype(BF16)


def mine_kernel(x_hbm, d_hbm, out_ref, x_ref, d_ref, sems):
    core = lax.axis_index("node") % 2
    loads = [
        pltpu.make_async_copy(x_hbm, x_ref, sems.at[0]),
        pltpu.make_async_copy(d_hbm, d_ref, sems.at[1]),
    ]
    for load in loads:
        load.start()
    turned = []
    for load, piece_ref in zip(loads, (x_ref, d_ref)):
        load.wait()
        turned.append(piece_ref[...].T.reshape(len(NODES), -1, 128))
    for spot, node in enumerate(NODES):
        x, d = turned[0][node], turned[1][node]
        out_ref[spot, :, 0:128] = jnp.where(core == 0, x, d)
        out_ref[spot, :, 128:256] = jnp.where(core == 0, d, x)


def other_ids(beside_ref):
    return beside_ref[len(NODES), 0:16, :].astype(F32)[0:1]


def partial_kernel(ids_ref, table_ref, mine_ref, beside_ref, out_ref):
    count, half, _ = table_ref.shape
    table = table_ref[...].reshape(count * half, 128)
    parts = []
    for ids, tile_ref in ((ids_ref[...].astype(F32), mine_ref), (other_ids(beside_ref), beside_ref)):
        both = jnp.zeros((64, 128), F32)
        for side in range(2):
            features = tile_ref[0:count, half * side : half * side + half, 0:128]
            wide = lax.dot_general(
                table,
                features.reshape(count * half, 128),
                (((0,), (0,)), ((), ())),
                preferred_element_type=F32,
            )
            both = both + wide[64 * side : 64 * side + 64]
        parts.append(jnp.where(ids == 0, both[0:32], both[32:64]))
    sums = jnp.concatenate(parts, axis=0).astype(BF16)
    out_ref[...] = jnp.broadcast_to(sums[None], out_ref.shape)


def by_adapter(ids, values):
    none = jnp.zeros_like(values)
    first = ids == 0
    return [jnp.where(first, values, none), jnp.where(first, none, values)]


def gradient_kernel(ids_ref, sums_ref, marked_ref, mine_ref, beside_ref, out_ref):
    core = lax.axis_index("node") % 2
    total = jnp.sum(sums_ref[...].astype(F32), axis=0)
    total = (total * jnp.where(core == 0, SCALE_IN, SCALE_RANK)).astype(BF16).astype(F32)
    count, half, _ = out_ref.shape
    grads = jnp.zeros((count * 2 * half, 128), F32)
    tiles = (
        (ids_ref[...].astype(F32), mine_ref[:, :, 128:256]),
        (other_ids(marked_ref), beside_ref[...]),
    )
    for spot, (ids, tile) in enumerate(tiles):
        halves = by_adapter(ids, total[32 * spot : 32 * spot + 32])
        grads = grads + lax.dot_general(
            tile.reshape(count * 2 * half, 128),
            jnp.concatenate(halves * 2, axis=0).astype(BF16),
            (((1,), (1,)), ((), ())),
            preferred_element_type=F32,
        )
    grads = grads * jnp.where(core == 0, SCALE_RANK, SCALE_IN)
    grads = grads.reshape(count, 2, half, 128)
    lane = lax.broadcasted_iota(jnp.int32, (1, 1, 128), 2)
    grads = jnp.where(lane < 64, grads[:, 0], grads[:, 1]).astype(BF16)
    for spot, node in enumerate(LAST_NODES):
        out_ref[spot] = grads[NODES.index(node)]


def grad_input_kernel(ids_ref, sums_ref, other_sums_ref, own_ref, other_ref, out_ref, table_ref):
    core = lax.axis_index("node") % 2
    lane = lax.broadcasted_iota(jnp.int32, (1, 128), 1)
    for spot, node in enumerate(NODES):
        block = jnp.where(core == 0, own_ref[spot], other_ref[spot])
        none = jnp.zeros_like(block)
        table_ref[node, 0] = jnp.where(lane < 64, block, none)
        table_ref[node, 1] = jnp.where(lane < 64, none, block)
    terms = jnp.where(core == 0, other_sums_ref[:, 32:64, :], sums_ref[:, 0:32, :])
    total = jnp.sum(terms.astype(F32), axis=0)
    back = (total * SCALE_RANK).astype(BF16).astype(F32)
    placed = jnp.concatenate(by_adapter(ids_ref[...], back) * 2, axis=0)
    table = table_ref[...].reshape(out_ref.shape[1], 128)
    grad = lax.dot_general(
        placed.T.astype(BF16), table, (((1,), (1,)), ((), ())), preferred_element_type=F32
    )
    out_ref[...] = (grad * SCALE_IN).astype(BF16)


def update_kernel(
    terms_ref, wd_ref, wu_ref, md_ref, vd_ref, mu_ref, vu_ref, down_ref, up_ref
):
    terms = terms_ref[...].astype(F32)
    terms = terms.reshape(terms.shape[0] // 2, 2, *terms.shape[1:])
    total = jnp.sum(terms, axis=0)
    sums = [jnp.concatenate([both[:, 0:64], both[:, 64:128]], axis=0) for both in total]
    for adapter in range(wd_ref.shape[0]):
        grad_a = sums[1][:, 32 * adapter : 32 * adapter + 32]
        grad_b = sums[0][:, 32 * adapter : 32 * adapter + 32].T
        down_ref[adapter] = moment_optimizer_step(
            wd_ref[adapter], grad_a, md_ref[adapter], vd_ref[adapter]
        )
        up_ref[adapter] = moment_optimizer_step(
            wu_ref[adapter], grad_b, mu_ref[adapter], vu_ref[adapter]
        )


def call(kernel, out_shape, *args, scratch=()):
    many = isinstance(out_shape, tuple)
    return pl.pallas_call(
        kernel,
        out_shape=out_shape,
        in_specs=[VMEM] * len(args),
        out_specs=(VMEM,) * len(out_shape) if many else VMEM,
        scratch_shapes=scratch,
        compiler_params=pltpu.CompilerParams(vmem_limit_bytes=16 * 2**20),
    )(*args)


def shape(dims, dtype):
    return jax.ShapeDtypeStruct(dims, dtype)


def exchange(blocks, axis, groups=None):
    return lax.all_to_all(
        blocks, axis, split_axis=0, concat_axis=0, axis_index_groups=groups, tiled=True
    )


def local(
    inputs,
    upstream,
    token_adapter_index,
    down_matrices,
    up_matrices,
    down_first_moment,
    down_second_moment,
    up_first_moment,
    up_second_moment,
):
    nodes = lax.axis_size("node")
    shards = lax.axis_size("tensor")
    depth = down_matrices.shape[1]
    def swap(block):
        return lax.ppermute(block, "node", [(node, node ^ 1) for node in range(nodes)])

    ids = token_adapter_index.reshape(1, 128)
    packed = pl.pallas_call(
        pack_kernel,
        out_shape=shape((nodes, depth // 2, 128), BF16),
        in_specs=[pl.BlockSpec(memory_space=pl.ANY)] * 2,
        out_specs=VMEM,
        scratch_shapes=[
            pltpu.VMEM(down_matrices.shape, F32),
            pltpu.VMEM(up_matrices.shape, F32),
            pltpu.SemaphoreType.DMA((2,)),
        ],
        compiler_params=pltpu.CompilerParams(vmem_limit_bytes=16 * 2**20),
    )(
        pltpu.with_memory_space_constraint(down_matrices, pltpu.HBM),
        pltpu.with_memory_space_constraint(up_matrices, pltpu.HBM),
    )
    own = exchange(packed, "node", [list(NODES)])
    rows = inputs.shape[0]
    whole = pltpu.VMEM(inputs.shape, BF16)

    def turn(kernel, dims, scratch, *small, flops=0):
        return pl.pallas_call(
            kernel,
            out_shape=shape(dims, BF16),
            in_specs=[pl.BlockSpec(memory_space=pl.ANY)] * (len(small) + 2),
            out_specs=VMEM,
            scratch_shapes=[*scratch, pltpu.SemaphoreType.DMA((2,))],
            compiler_params=pltpu.CompilerParams(vmem_limit_bytes=16 * 2**20),
            cost_estimate=pl.CostEstimate(
                flops=flops, bytes_accessed=2**20, transcendentals=0
            ),
        )(
            *(pltpu.with_memory_space_constraint(one, pltpu.HBM) for one in small),
            pltpu.with_memory_space_constraint(inputs, pltpu.HBM),
            pltpu.with_memory_space_constraint(upstream, pltpu.HBM),
        )

    def away(second):
        dims = (nodes + 1 - second, depth, rows)
        scratch = [whole, pltpu.VMEM(ids.shape, jnp.int32)]
        return swap(turn(functools.partial(away_kernel, second), dims, scratch, ids))

    beside, rest = away(0), away(1)
    mine = turn(mine_kernel, (nodes, depth, 2 * rows), [whole, whole], flops=NEAR_FLOPS)
    own, mine = lax.optimization_barrier((own, mine))
    beside, rest = lax.optimization_barrier((beside, rest))
    parts = call(partial_kernel, shape((shards, 64, 128), BF16), ids, own, mine, beside)
    sums = exchange(parts, "tensor", [list(ALONG_TENSOR)])
    other = swap(own)
    terms = call(
        gradient_kernel, shape((nodes, depth // 2, 128), BF16), ids, sums, beside, mine, rest
    )
    terms = exchange(terms, "node", [list(LAST_NODES)])
    grad_in = call(
        grad_input_kernel,
        shape(inputs.shape, BF16),
        ids,
        sums,
        swap(sums),
        own,
        other,
        scratch=[pltpu.VMEM((nodes, 2, depth // 2, 128), BF16)],
    )
    down, up = call(
        update_kernel,
        (shape(down_matrices.shape, F32), shape(up_matrices.shape, F32)),
        terms,
        down_matrices,
        up_matrices,
        down_first_moment,
        down_second_moment,
        up_first_moment,
        up_second_moment,
    )
    return (grad_in, down, up)


def solution(mesh):
    return jax.shard_map(
        local,
        mesh=mesh,
        in_specs=(
            P("node", "tensor"),
            P("node", "tensor"),
            P("node"),
            P(None, ("tensor", "node"), None),
            P(None, None, ("tensor", "node")),
            P(None, ("tensor", "node"), None),
            P(None, ("tensor", "node"), None),
            P(None, None, ("tensor", "node")),
            P(None, None, ("tensor", "node")),
        ),
        out_specs=(
            P("node", "tensor"),
            P(None, ("tensor", "node"), None),
            P(None, None, ("tensor", "node")),
        ),
        check_vma=False,
    )
```
